256 devices in a mesh: row: 16 (over z, core), col: 4 (over y), rep: 4 (over x).
Axes of the slice: x: 4, y: 4, z: 8, core: 2. Of those that a mesh axis runs over, the one named last changes fastest.
Arguments:
- density: bfloat16 [8192, 8192], P('row', 'col'), may hold values from -1.5 to 1.75, as said below
- pattern_density: int32 [256, 256], P('row', 'col'), may hold values 0 or 1
- pattern_square: int32 [256, 256], P('row', 'col'), may hold values 0 or 1
- pattern_cube: int32 [256, 256], P('row', 'col'), may hold values 0 or 1
Outputs:
- purified: bfloat16 [8192, 8192], P('row', ('col', 'rep'))
The draws below stay inside these ranges and needn't reach their ends.
Inputs may be any that keep to these rules, and one draw needn't show every extreme that they name: `density`: symmetric.
All inputs are finite; a program needn't handle non-finite values. No bound on the sum of `pattern_density` or of `pattern_square` or of `pattern_cube` on one device may be relied on, other than what follows from the above.
Results may differ from the reference program's by a relative error of at most 0.0054.
Values may be sent and summed in bfloat16 or wider, within the bound.
No kernel may reach another device: no remote copies, remote signals or barrier semaphores. Data moves between devices by JAX's collectives and lax.ppermute only.
A program may use at most 64 MiB of HBM per device.

```python
import jax
import jax.numpy as jnp
from jax import lax

BLK = 32
NB = 256
ORDER = 8192


def draw_density(key, part):
    key = jax.random.fold_in(key, 11)
    key_noise = jax.random.fold_in(key, 0)
    noise = jnp.clip(jax.random.normal(key_noise, (ORDER, ORDER), jnp.float32), -5.0, 5.0)
    symmetric = 0.5 * (noise + noise.T)
    diagonal = (lax.broadcasted_iota(jnp.int32, (ORDER, ORDER), 0) == lax.broadcasted_iota(jnp.int32, (ORDER, ORDER), 1)).astype(jnp.float32)
    return (0.5 * diagonal + 0.5 * ORDER ** (-0.5) * symmetric).astype(jnp.bfloat16)


def touch_ends(array, stream_key, smallest, top_value):
    longest = array.shape.index(max(array.shape))
    spots = []
    for shift in (0, 1):
        where = [jax.random.randint(jax.random.fold_in(stream_key, axis), (), 0, length) for axis, length in enumerate(array.shape)]
        where[longest] = (where[longest] + shift) % array.shape[longest]
        spots.append(tuple(where))
    return array.at[spots[0]].set(smallest).at[spots[1]].set(top_value)


def setup_inputs(seed: int = 0) -> dict:
    arg_keys = jax.random.split(jax.random.key(seed), 5)
    return {
        "density": draw_density(jax.random.fold_in(arg_keys[4], 71), 0),
        "pattern_density": touch_ends((jax.random.randint(arg_keys[1], (NB, NB), 0, 4) < 3).astype(jnp.int32), jax.random.fold_in(arg_keys[1], 1), 0, 1),
        "pattern_square": touch_ends((jax.random.randint(arg_keys[2], (NB, NB), 0, 4) < 3).astype(jnp.int32), jax.random.fold_in(arg_keys[2], 1), 0, 1),
        "pattern_cube": touch_ends((jax.random.randint(arg_keys[3], (NB, NB), 0, 4) < 3).astype(jnp.int32), jax.random.fold_in(arg_keys[3], 1), 0, 1),
    }


def spread(pattern):
    wide = jnp.repeat(jnp.repeat(pattern, BLK, axis=0), BLK, axis=1)
    return wide > 0


def reference(density, pattern_density, pattern_square, pattern_cube):
    masked = jnp.where(spread(pattern_density), density, jnp.zeros_like(density)).astype(jnp.float32)
    product_one = jnp.dot(masked, masked, precision=lax.Precision.HIGHEST, preferred_element_type=jnp.float32)
    square = jnp.where(spread(pattern_square), product_one, jnp.float32(0.0)).astype(jnp.bfloat16)
    product_two = jnp.dot(square.astype(jnp.float32), masked, precision=lax.Precision.HIGHEST, preferred_element_type=jnp.float32)
    cube = jnp.where(spread(pattern_cube), product_two, jnp.float32(0.0))
    return (3.0 * square.astype(jnp.float32) - 2.0 * cube).astype(jnp.bfloat16)
```

```python
import functools

import jax
import jax.numpy as jnp
from jax import lax
from jax.experimental import pallas as pl
from jax.experimental.pallas import tpu as pltpu
from jax.sharding import PartitionSpec as P

BLK = 32
BF = jnp.bfloat16
F32 = jnp.float32
VMEM = pl.BlockSpec(memory_space=pltpu.VMEM)
SMEM = pl.BlockSpec(memory_space=pltpu.SMEM)
NT = (((1,), (1,)), ((), ()))
NN = (((1,), (0,)), ((), ()))

SLOTS = (0, -1, 1, -2, 2, -3, 3, 4)
CHUNKS = ((0, 1, 2), (3, 4), (5, 6), (7,))
PHASES = ((0, 1), (2, 3))


def call(kernel, out_shape, n_in, scratch=(), flops=0, byts=0):
    return pl.pallas_call(
        kernel,
        out_shape=out_shape,
        in_specs=[SMEM] + [VMEM] * (n_in - 1),
        out_specs=jax.tree.map(lambda _: VMEM, out_shape),
        scratch_shapes=list(scratch),
        compiler_params=pltpu.CompilerParams(vmem_limit_bytes=56 << 20),
        cost_estimate=pl.CostEstimate(flops=flops, bytes_accessed=byts, transcendentals=0),
    )


def shape(*dims, dtype=BF):
    return jax.ShapeDtypeStruct(dims, dtype)


def iota(dims, axis):
    return lax.broadcasted_iota(jnp.int32, dims, axis)


def dot(a, b, dims=NN):
    return lax.dot_general(a, b, dims, preferred_element_type=F32)


def row_of_slot(index, z, core, layer):
    slot = index // 8
    other = (index // 4) % 2
    offset = jnp.where(slot == 7, 4, jnp.where(slot % 2 == 1, -((slot + 1) // 2), slot // 2))
    chip = lax.rem(z + offset + 8, 8)
    band = 2 * chip + lax.rem(core + other, 2)
    return 16 * band + 4 * layer + index % 4


def prep_kernel(s_ref, pat_ref, sq_ref, dloc_ref, cu_ref, density_ref, left_ref, mk_ref, mt_ref, ms_ref, mc_ref):
    z, core, col, layer = s_ref[0], s_ref[1], s_ref[2], s_ref[3]
    pick = (row_of_slot(iota((64, 256), 0), z, core, layer) == iota((64, 256), 1)).astype(BF)
    own_cols = (iota((256, 2048), 0) == 64 * col + iota((256, 2048), 1) // BLK).astype(BF)
    wide = (iota((64, 2048), 0) == iota((64, 2048), 1) // BLK).astype(BF)
    roll = (iota((16, 16), 1) == lax.rem(iota((16, 16), 0) + 4 * col, 16)).astype(BF)
    mk_ref[...] = dot(dot(pick, pat_ref[...]).astype(BF), own_cols).astype(BF)
    transposed = dot(pick, pat_ref[pl.ds(pl.multiple_of(64 * col, 64), 64), :], NT).astype(BF)
    mt_ref[...] = dot(transposed, wide).astype(BF)
    square = dot(dot(roll, sq_ref[...]).astype(BF), pick, NT).astype(BF)
    ms_ref[...] = dot(square, wide).astype(BF)
    mc_ref[...] = dot(dot(roll, cu_ref[...]).astype(BF), wide)
    local = dot(dot(roll, dloc_ref[...]).astype(BF), wide).astype(BF)
    for quarter in range(4):
        start = pl.multiple_of(128 * lax.rem(col + quarter, 4), 128)
        for block in range(4):
            row = 4 * quarter + block
            left_ref[pl.ds(BLK * row, BLK), :] = (
                density_ref[pl.ds(start + BLK * block, BLK), :] * local[row : row + 1, :]
            )


def load_pieces(piece_refs, mask_ref, block_row, out_ref):
    done = 0
    for ref in piece_refs:
        for block in range(ref.shape[0] // BLK):
            row = block_row + done // BLK
            out_ref[pl.ds(done, BLK), :] = ref[pl.ds(BLK * block, BLK), :] * mask_ref[pl.ds(row, 1), :]
            done += BLK


def product_one_kernel(block_row, n_pieces, s_ref, left_ref, mt_ref, *refs):
    pieces, (own_ref, *send_refs), right = refs[:n_pieces], refs[n_pieces:-1], refs[-1]
    load_pieces(pieces, mt_ref, block_row, right)
    for start in range(0, right.shape[0], 256):
        block = dot(left_ref[...], right[pl.ds(start, 256), :], NT)
        own_ref[:, pl.ds(start, 256)] = block[:128]
        for quarter in range(3):
            rows = 128 * (quarter + 1)
            send_refs[quarter][:, pl.ds(start, 256)] = block[rows : rows + 128].astype(BF)


def square_kernel(block_row, s_ref, own_ref, a_ref, b_ref, c_ref, ms_ref, out_ref):
    width = out_ref.shape[1]
    total = own_ref[...] + a_ref[...].astype(F32) + b_ref[...].astype(F32) + c_ref[...].astype(F32)
    for block in range(4):
        rows = slice(BLK * block, BLK * block + BLK)
        keep = ms_ref[pl.ds(block, 1), pl.ds(BLK * block_row, width)].astype(F32)
        out_ref[rows, :] = (total[rows] * keep).astype(BF)


def product_two_kernel(chunks, n_pieces, last, s_ref, mk_ref, mc_ref, *refs):
    z, core, col, layer = s_ref[0], s_ref[1], s_ref[2], s_ref[3]
    refs = list(refs)
    right, square, total = refs[-3:]
    before = refs.pop(0) if last else None
    squares, refs = refs[: 4 * len(chunks)], refs[4 * len(chunks) :]
    pieces, outs = refs[:n_pieces], refs[n_pieces:-3]
    slots = [slot for chunk in chunks for slot in CHUNKS[chunk]]
    load_pieces(pieces, mk_ref, 8 * slots[0], right)
    start = 0
    for n in range(len(chunks)):
        for quarter in range(4):
            ref = squares[4 * n + quarter]
            square[pl.ds(128 * quarter, 128), pl.ds(start, ref.shape[1])] = ref[...]
        start += squares[4 * n].shape[1]
    if not last:
        total = outs[0]
    for cols in range(0, 2048, 256):
        block = dot(square[...], right[:, pl.ds(cols, 256)])
        for row in range(16):
            rows = slice(BLK * row, BLK * row + BLK)
            part = block[rows] * (-2.0 * mc_ref[pl.ds(row, 1), pl.ds(cols, 256)])
            if last:
                part = part + before[rows, pl.ds(cols, 256)]
            total[rows, pl.ds(cols, 256)] = part
    for n, slot in enumerate(slots):
        chip = lax.rem(z + SLOTS[slot] + 8, 8)

        @pl.when(chip // 2 == col)
        def _():
            for other in range(2):
                band = 2 * chip + lax.rem(core + other, 2) - 4 * col
                cols = pl.ds(pl.multiple_of(512 * band + 128 * layer, 128), 128)
                total[:, cols] += 3.0 * square[:, pl.ds(256 * n + 128 * other, 128)].astype(F32)

    if last:
        for share in range(4):
            cols = pl.ds(pl.multiple_of(512 * lax.rem(layer + share, 4), 512), 512)
            outs[share][...] = total[:, cols].astype(outs[share].dtype)


def finish_kernel(s_ref, own_ref, a_ref, b_ref, c_ref, out_ref):
    col = s_ref[2]
    for quarter in range(4):
        rows = slice(128 * quarter, 128 * quarter + 128)
        total = own_ref[rows] + a_ref[rows].astype(F32) + b_ref[rows].astype(F32) + c_ref[rows].astype(F32)
        out_ref[pl.ds(pl.multiple_of(128 * lax.rem(col + quarter, 4), 128), 128), :] = total.astype(BF)


def shift(array, axis, step, size):
    return lax.ppermute(array, axis, [(i, (i + step) % size) for i in range(size)])


def swap(array):
    return lax.ppermute(array, "row", [(i, i ^ 1) for i in range(16)])


def exchange(parts, axis):
    got = [shift(part, axis, step, 4) for part, step in zip(parts, (1, 2, 3))]
    return got[2], got[1], got[0]


def body(density, pattern_density, pattern_square, pattern_cube):
    row, col, layer = lax.axis_index("row"), lax.axis_index("col"), lax.axis_index("rep")
    where = jnp.stack([row // 2, row % 2, col, layer]).astype(jnp.int32)
    own = lax.dynamic_slice_in_dim(density, 128 * layer, 128, 0)

    both = jnp.concatenate([pattern_density, pattern_square], 0).astype(BF)
    band = lax.all_gather(both, "col", axis=1, tiled=True)
    whole = lax.all_gather(band[:16], "row", axis=0, tiled=True)

    up, down = [own], [own]
    for step in range(1, 5):
        first, second = up[-1], down[-1]
        if step == 4:
            first, second = first[:64], second[64:]
        up.append(shift(first, "row", 2, 16))
        down.append(shift(second, "row", -2, 16))
    held = {0: [own], 4: [up[4], down[4]]}
    for step in (1, 2, 3):
        held[-step], held[step] = [up[step]], [down[step]]
    pieces = []
    for offset in SLOTS:
        pieces.append(held[offset] + [swap(piece) for piece in held[offset]])

    left, mk, mt, ms, mc = call(
        prep_kernel,
        (shape(512, 2048), shape(64, 2048), shape(64, 2048), shape(16, 2048), shape(16, 2048, dtype=F32)),
        6,
        flops=2 * 300 * 256 * 2048,
        byts=6 << 20,
    )(where, whole, band[16:], pattern_density.astype(BF), pattern_cube.astype(BF), density)

    squares = []
    for slots in CHUNKS:
        width = 256 * len(slots)
        held = [piece for slot in slots for piece in pieces[slot]]
        mine, *others = call(
            functools.partial(product_one_kernel, 8 * slots[0], len(held)),
            (shape(128, width, dtype=F32), shape(128, width), shape(128, width), shape(128, width)),
            3 + len(held),
            [pltpu.VMEM((width, 2048), BF)],
            flops=2 * 512 * 2048 * width,
            byts=2 * 2048 * (512 + width),
        )(where, left, mt, *held)
        got = exchange(others, "col")
        mine = call(
            functools.partial(square_kernel, 8 * slots[0]),
            shape(128, width),
            6,
            byts=2 * 128 * width * 6,
        )(where, mine, *got, ms)
        squares.append((mine, *exchange([mine] * 3, "col")))

    total = []
    for number, chunks in enumerate(PHASES):
        last = number == len(PHASES) - 1
        held = [piece for chunk in chunks for slot in CHUNKS[chunk] for piece in pieces[slot]]
        blocks = [block for chunk in chunks for block in squares[chunk]]
        width = sum(squares[chunk][0].shape[1] for chunk in chunks)
        if last:
            out = (shape(512, 512, dtype=F32), shape(512, 512), shape(512, 512), shape(512, 512))
        else:
            out = (shape(512, 2048, dtype=F32),)
        total = call(
            functools.partial(product_two_kernel, chunks, len(held), last),
            out,
            3 + len(total) + len(blocks) + len(held),
            [
                pltpu.VMEM((width, 2048), BF),
                pltpu.VMEM((512, width), BF),
                pltpu.VMEM((512 if last else 8, 2048), F32),
            ],
            flops=2 * 512 * 2048 * width,
            byts=2 * 2048 * (1024 + width),
        )(where, mk, mc, *total, *blocks, *held)
    mine, *others = total
    return call(finish_kernel, shape(512, 512), 5, byts=3 << 20)(where, mine, *exchange(others, "rep"))


def solution(mesh):
    placed = (P("row", "col"), P("row", "col"), P("row", "col"), P("row", "col"))
    return jax.shard_map(
        body, mesh=mesh, in_specs=placed, out_specs=P("row", ("col", "rep")), check_vma=False
    )
```

```python
import functools

import jax
import jax.numpy as jnp
from jax import lax
from jax.experimental import pallas as pl
from jax.experimental.pallas import tpu as pltpu
from jax.sharding import PartitionSpec as P

BLK = 32
BF = jnp.bfloat16
F32 = jnp.float32
VMEM = pl.BlockSpec(memory_space=pltpu.VMEM)
SMEM = pl.BlockSpec(memory_space=pltpu.SMEM)
NT = (((1,), (1,)), ((), ()))
NN = (((1,), (0,)), ((), ()))

SLOTS = (0, -1, 1, -2, 2, -3, 3, 4)
CHUNKS = ((0, 1, 2), (3, 4), (5, 6), (7,))
PHASES = ((0, 1, 2), (3,))


def call(kernel, out_shape, n_in, scratch=(), flops=0, byts=0):
    return pl.pallas_call(
        kernel,
        out_shape=out_shape,
        in_specs=[SMEM] + [VMEM] * (n_in - 1),
        out_specs=jax.tree.map(lambda _: VMEM, out_shape),
        scratch_shapes=list(scratch),
        compiler_params=pltpu.CompilerParams(vmem_limit_bytes=56 << 20),
        cost_estimate=pl.CostEstimate(flops=flops, bytes_accessed=byts, transcendentals=0),
    )


def shape(*dims, dtype=BF):
    return jax.ShapeDtypeStruct(dims, dtype)


def iota(dims, axis):
    return lax.broadcasted_iota(jnp.int32, dims, axis)


def dot(a, b, dims=NN):
    return lax.dot_general(a, b, dims, preferred_element_type=F32)


def row_of_slot(index, z, core, layer):
    slot = index // 8
    other = (index // 4) % 2
    offset = jnp.where(slot == 7, 4, jnp.where(slot % 2 == 1, -((slot + 1) // 2), slot // 2))
    chip = lax.rem(z + offset + 8, 8)
    band = 2 * chip + lax.rem(core + other, 2)
    return 16 * band + 4 * layer + index % 4


def prep_kernel(s_ref, *refs):
    whole_refs, both_refs, (local_ref, cube_ref, density_ref) = refs[:4], refs[4:8], refs[8:11]
    left_ref, mk_ref, mt_ref, ms_ref, mc_ref, whole = refs[11:]
    z, core, col, layer = s_ref[0], s_ref[1], s_ref[2], s_ref[3]
    row = 2 * z + core
    wide = (iota((64, 2048), 0) == iota((64, 2048), 1) // BLK).astype(BF)
    roll = (iota((16, 16), 1) == lax.rem(iota((16, 16), 0) + 4 * col, 16)).astype(BF)
    local = dot(dot(roll, local_ref[...].astype(BF)).astype(BF), wide).astype(BF)
    for quarter in range(4):
        start = pl.multiple_of(128 * lax.rem(col + quarter, 4), 128)
        for block in range(4):
            at = 4 * quarter + block
            left_ref[pl.ds(BLK * at, BLK), :] = (
                density_ref[pl.ds(start + BLK * block, BLK), :] * local[at : at + 1, :]
            )
    for n in range(4):
        whole[pl.ds(256 * n, 256), :] = whole_refs[n][...]
    at = iota((64, 1024), 1)
    band = 4 * lax.rem(row // 4 + at // 256, 4) + lax.rem(row % 4 + (at // 64) % 4, 4)
    block_row, turn = 16 * band + at % 16, (at // 16) % 4
    share = row_of_slot(iota((64, 1024), 0), z, core, layer)
    pick = jnp.where((block_row == share) & (turn == 0), 1.0, 0.0).astype(BF)
    mk = dot(pick, whole[...]).astype(BF)
    mine = block_row == 64 * col + iota((64, 1024), 0)
    mt = jnp.zeros((64, 64), F32)
    ms = jnp.zeros((16, 64), F32)
    for n in range(4):
        rows = dot(jnp.where(mine & (turn == n), 1.0, 0.0).astype(BF), whole[...]).astype(BF)
        column = 64 * lax.rem(col + n, 4) + iota((64, 64), 1)
        take = (column == row_of_slot(iota((64, 64), 0), z, core, layer)).astype(BF)
        mt = mt + dot(take, rows, NT)
        ms = ms + dot(dot(roll, both_refs[n][pl.ds(16, 16), :]).astype(BF), take, NT)
    mk_ref[...] = dot(mk, wide)
    mt_ref[...] = dot(mt.astype(BF), wide)
    ms_ref[...] = dot(ms.astype(BF), wide)
    mc_ref[...] = -2.0 * dot(dot(roll, cube_ref[...].astype(BF)).astype(BF), wide)


def load_pieces(piece_refs, mask_ref, block_row, out_ref):
    done = 0
    for ref in piece_refs:
        for block in range(ref.shape[0] // BLK):
            row = block_row + done // BLK
            keep = jnp.broadcast_to(mask_ref[pl.ds(row, 1), :], (BLK, 2048)).astype(BF)
            out_ref[pl.ds(done, BLK), :] = ref[pl.ds(BLK * block, BLK), :] * keep
            done += BLK


def stage_kernel(before, now, n_pieces, s_ref, *refs):
    refs = list(refs)
    take = lambda n: [refs.pop(0) for _ in range(n)]
    start = width = 0
    if before is not None:
        ms_ref, own_ref, *got = take(5)
        width = own_ref.shape[1]
        skip = got[0].shape[1] - width
    if now is not None:
        left_ref, mt_ref = take(2)
        pieces = take(n_pieces)
    outs = take(3)
    if before is not None:
        (square_ref,) = take(1)
        first = 256 * CHUNKS[before][0]
        total = own_ref[...]
        for ref in got:
            total = total + ref[:, pl.ds(skip, width)].astype(F32)
        for block in range(4):
            rows = slice(BLK * block, BLK * block + BLK)
            kept = (total[rows] * ms_ref[pl.ds(block, 1), pl.ds(first, width)]).astype(BF)
            square_ref[rows, :] = kept
            for out in outs:
                out[rows, pl.ds(0, width)] = kept
    if now is not None:
        partial_ref, right = take(2)
        load_pieces(pieces, mt_ref, 8 * CHUNKS[now][0], right)
        for start in range(0, right.shape[0], 256):
            block = dot(left_ref[...], right[pl.ds(start, 256), :], NT)
            partial_ref[:, pl.ds(start, 256)] = block[:128]
            for quarter in range(3):
                rows = 128 * (quarter + 1)
                outs[quarter][:, pl.ds(width + start, 256)] = block[rows : rows + 128].astype(BF)


def product_two_kernel(chunks, n_pieces, last, s_ref, mk_ref, mc_ref, *refs):
    z, core, col, layer = s_ref[0], s_ref[1], s_ref[2], s_ref[3]
    refs = list(refs)
    right, square, total = refs[-3:]
    before = refs.pop(0) if last else None
    squares, refs = refs[: 4 * len(chunks)], refs[4 * len(chunks) :]
    pieces, outs = refs[:n_pieces], refs[n_pieces:-3]
    slots = [slot for chunk in chunks for slot in CHUNKS[chunk]]
    load_pieces(pieces, mk_ref, 8 * slots[0], right)
    start = 0
    for n in range(len(chunks)):
        width = squares[4 * n].shape[1]
        for quarter in range(4):
            square[pl.ds(128 * quarter, 128), pl.ds(start, width)] = squares[4 * n + quarter][:, pl.ds(0, width)]
        start += width
    if not last:
        total = outs[0]
    for cols in range(0, 2048, 256):
        block = dot(square[...], right[:, pl.ds(cols, 256)])
        for row in range(16):
            rows = slice(BLK * row, BLK * row + BLK)
            part = block[rows] * mc_ref[pl.ds(row, 1), pl.ds(cols, 256)]
            if last:
                part = part + before[rows, pl.ds(cols, 256)]
            total[rows, pl.ds(cols, 256)] = part
    for n, slot in enumerate(slots):
        chip = lax.rem(z + SLOTS[slot] + 8, 8)

        @pl.when(chip // 2 == col)
        def _():
            for other in range(2):
                band = 2 * chip + lax.rem(core + other, 2) - 4 * col
                cols = pl.ds(pl.multiple_of(512 * band + 128 * layer, 128), 128)
                total[:, cols] += 3.0 * square[:, pl.ds(256 * n + 128 * other, 128)].astype(F32)

    if last:
        for share in range(4):
            cols = pl.ds(pl.multiple_of(512 * lax.rem(layer + share, 4), 512), 512)
            outs[share][...] = total[:, cols].astype(outs[share].dtype)


def finish_kernel(s_ref, own_ref, a_ref, b_ref, c_ref, out_ref):
    col = s_ref[2]
    for quarter in range(4):
        rows = slice(128 * quarter, 128 * quarter + 128)
        total = own_ref[rows] + a_ref[rows].astype(F32) + b_ref[rows].astype(F32) + c_ref[rows].astype(F32)
        out_ref[pl.ds(pl.multiple_of(128 * lax.rem(col + quarter, 4), 128), 128), :] = total.astype(BF)


def shift(array, axis, step, size):
    return lax.ppermute(array, axis, [(i, (i + step) % size) for i in range(size)])


def swap(array):
    return lax.ppermute(array, "row", [(i, i ^ 1) for i in range(16)])


def exchange(parts, axis):
    got = [shift(part, axis, step, 4) for part, step in zip(parts, (1, 2, 3))]
    return got[2], got[1], got[0]


def gather_patterns(pattern_density, pattern_square):
    both = jnp.concatenate([pattern_density, pattern_square], 0).astype(BF)
    cols = [both, *exchange([both] * 3, "col")]
    rows = jnp.concatenate([part[:16] for part in cols], 0)
    near = [lax.ppermute(rows, "row", [(i, i // 4 * 4 + (i + step) % 4) for i in range(16)]) for step in (3, 2, 1)]
    rows = jnp.concatenate([rows, *near], 0)
    far = [shift(rows, "row", 4 * step, 16) for step in (3, 2, 1)]
    return [rows, *far], cols


def body(density, pattern_density, pattern_square, pattern_cube):
    row, col, layer = lax.axis_index("row"), lax.axis_index("col"), lax.axis_index("rep")
    where = jnp.stack([row // 2, row % 2, col, layer]).astype(jnp.int32)
    own = lax.dynamic_slice_in_dim(density, 128 * layer, 128, 0)

    up, down = [own], [own]
    for step in range(1, 5):
        first, second = up[-1], down[-1]
        if step == 4:
            first, second = first[:64], second[64:]
        up.append(shift(first, "row", 2, 16))
        down.append(shift(second, "row", -2, 16))
    held = {0: [own], 4: [up[4], down[4]]}
    for step in (1, 2, 3):
        held[-step], held[step] = [up[step]], [down[step]]
    pieces = []
    for offset in SLOTS:
        pieces.append(held[offset] + [swap(piece) for piece in held[offset]])

    whole, both = gather_patterns(pattern_density, pattern_square)
    left, mk, mt, ms, mc = call(
        prep_kernel,
        (
            shape(512, 2048),
            shape(64, 2048, dtype=F32),
            shape(64, 2048, dtype=F32),
            shape(16, 2048, dtype=F32),
            shape(16, 2048, dtype=F32),
        ),
        12,
        [pltpu.VMEM((1024, 64), BF)],
        flops=2 * 200 * 256 * 2048,
        byts=6 << 20,
    )(where, *whole, *both, pattern_density, pattern_cube, density)

    squares, partial, got = [], None, None
    for number in range(len(CHUNKS) + 1):
        before = number - 1 if number > 0 else None
        now = number if number < len(CHUNKS) else None
        operands, outs, extra, scratch, held = [], [], [], [], []
        width = new = 0
        if before is not None:
            operands += [ms, partial, *got]
            width = partial.shape[1]
            extra.append(shape(128, width))
        if now is not None:
            new = 256 * len(CHUNKS[now])
            held = [piece for slot in CHUNKS[now] for piece in pieces[slot]]
            operands += [left, mt, *held]
            extra.append(shape(128, new, dtype=F32))
            scratch.append(pltpu.VMEM((new, 2048), BF))
        results = call(
            functools.partial(stage_kernel, before, now, len(held)),
            (shape(128, width + new),) * 3 + tuple(extra),
            1 + len(operands),
            scratch,
            flops=2 * 512 * 2048 * new,
            byts=2 * 2048 * (512 * (new > 0) + new),
        )(where, *operands)
        got = exchange(results[:3], "col")
        if before is not None:
            squares.append((results[3], *got))
        partial = results[-1]

    total = []
    for number, chunks in enumerate(PHASES):
        last = number == len(PHASES) - 1
        held = [piece for chunk in chunks for slot in CHUNKS[chunk] for piece in pieces[slot]]
        blocks = [block for chunk in chunks for block in squares[chunk]]
        width = sum(squares[chunk][0].shape[1] for chunk in chunks)
        if last:
            out = (shape(512, 512, dtype=F32), shape(512, 512), shape(512, 512), shape(512, 512))
        else:
            out = (shape(512, 2048, dtype=F32),)
        total = call(
            functools.partial(product_two_kernel, chunks, len(held), last),
            out,
            3 + len(total) + len(blocks) + len(held),
            [
                pltpu.VMEM((width, 2048), BF),
                pltpu.VMEM((512, width), BF),
                pltpu.VMEM((512 if last else 8, 2048), F32),
            ],
            flops=2 * 512 * 2048 * width,
            byts=2 * 2048 * (1024 + width),
        )(where, mk, mc, *total, *blocks, *held)
    mine, *others = total
    return call(finish_kernel, shape(512, 512), 5, byts=3 << 20)(where, mine, *exchange(others, "rep"))


def solution(mesh):
    placed = (P("row", "col"), P("row", "col"), P("row", "col"), P("row", "col"))
    return jax.shard_map(
        body, mesh=mesh, in_specs=placed, out_specs=P("row", ("col", "rep")), check_vma=False
    )
```

```python
import functools

import jax
import jax.numpy as jnp
from jax import lax
from jax.experimental import pallas as pl
from jax.experimental.pallas import tpu as pltpu
from jax.sharding import PartitionSpec as P

BLK = 32
BF = jnp.bfloat16
F32 = jnp.float32
VMEM = pl.BlockSpec(memory_space=pltpu.VMEM)
SMEM = pl.BlockSpec(memory_space=pltpu.SMEM)
NT = (((1,), (1,)), ((), ()))
NN = (((1,), (0,)), ((), ()))

SLOTS = (0, -1, 1, -2, 2, -3, 3, 4)
CHUNKS = ((0, 1, 2), (3, 4), (5, 6), (7,))
PHASES = ((0, 1), (2,), (3,))


def call(kernel, out_shape, n_in, scratch=(), flops=0, byts=0, mib=24, aliases={}):
    return pl.pallas_call(
        kernel,
        out_shape=out_shape,
        in_specs=[SMEM] + [VMEM] * (n_in - 1),
        out_specs=jax.tree.map(lambda _: VMEM, out_shape),
        scratch_shapes=list(scratch),
        input_output_aliases=aliases,
        compiler_params=pltpu.CompilerParams(vmem_limit_bytes=mib << 20),
        cost_estimate=pl.CostEstimate(flops=flops, bytes_accessed=byts, transcendentals=0),
    )


def shape(*dims, dtype=BF):
    return jax.ShapeDtypeStruct(dims, dtype)


def iota(dims, axis):
    return lax.broadcasted_iota(jnp.int32, dims, axis)


def dot(a, b, dims=NN):
    return lax.dot_general(a, b, dims, preferred_element_type=F32)


def row_of_slot(index, z, core, layer):
    slot = index // 8
    other = (index // 4) % 2
    offset = jnp.where(slot == 7, 4, jnp.where(slot % 2 == 1, -((slot + 1) // 2), slot // 2))
    chip = lax.rem(z + offset + 8, 8)
    band = 2 * chip + lax.rem(core + other, 2)
    return 16 * band + 4 * layer + index % 4


def prep_kernel(s_ref, *refs):
    both_refs, (local_ref, cube_ref, density_ref) = refs[:4], refs[4:7]
    left_ref, mk_ref, mt_ref, ms_ref, mc_ref = refs[7:]
    z, core, col, layer = s_ref[0], s_ref[1], s_ref[2], s_ref[3]
    wide = (iota((64, 2048), 0) == iota((64, 2048), 1) // BLK).astype(BF)
    roll = (iota((16, 16), 1) == lax.rem(iota((16, 16), 0) + 4 * col, 16)).astype(BF)
    local = dot(dot(roll, local_ref[...].astype(BF)).astype(BF), wide).astype(BF)
    for quarter in range(4):
        start = pl.multiple_of(128 * lax.rem(col + quarter, 4), 128)
        for block in range(4):
            at = 4 * quarter + block
            left_ref[pl.ds(BLK * at, BLK), :] = (
                density_ref[pl.ds(start + BLK * block, BLK), :] * local[at : at + 1, :]
            )
    at = iota((64, 256), 1)
    chip = lax.rem(z + lax.rem(layer + at // 64, 4) + 4 * ((at // 16) % 2), 8)
    block_row = 16 * (2 * chip + lax.rem(core + (at // 32) % 2, 2)) + at % 16
    share = row_of_slot(iota((64, 256), 0), z, core, layer)
    pick = jnp.where(block_row == share, 1.0, 0.0).astype(BF)
    mk = dot(pick, both_refs[0][pl.ds(0, 256), :]).astype(BF)
    mine = jnp.where(block_row == 64 * col + iota((64, 256), 0), 1.0, 0.0).astype(BF)
    mt = jnp.zeros((64, 64), F32)
    ms = jnp.zeros((16, 64), F32)
    for n in range(4):
        rows = dot(mine, both_refs[n][pl.ds(0, 256), :]).astype(BF)
        column = 64 * lax.rem(col + n, 4) + iota((64, 64), 1)
        take = (column == row_of_slot(iota((64, 64), 0), z, core, layer)).astype(BF)
        mt = mt + dot(take, rows, NT)
        ms = ms + dot(dot(roll, both_refs[n][pl.ds(256, 16), :]).astype(BF), take, NT)
    mk_ref[...] = dot(mk, wide)
    mt_ref[...] = dot(mt.astype(BF), wide)
    ms_ref[...] = dot(ms.astype(BF), wide)
    mc_ref[...] = -2.0 * dot(dot(roll, cube_ref[...].astype(BF)).astype(BF), wide)


def load_pieces(piece_refs, mask_ref, block_row, out_ref):
    done = 0
    for ref in piece_refs:
        for block in range(ref.shape[0] // BLK):
            row = block_row + done // BLK
            keep = jnp.broadcast_to(mask_ref[pl.ds(row, 1), :], (BLK, 2048)).astype(BF)
            out_ref[pl.ds(done, BLK), :] = ref[pl.ds(BLK * block, BLK), :] * keep
            done += BLK


def stage_kernel(before, now, n_pieces, s_ref, *refs):
    refs = list(refs)
    take = lambda n: [refs.pop(0) for _ in range(n)]
    start = width = 0
    if before is not None:
        ms_ref, own_ref, *got = take(5)
        width = own_ref.shape[1]
        skip = got[0].shape[1] - width
    if now is not None:
        left_ref, mt_ref = take(2)
        pieces = take(n_pieces)
    outs = take(3 if now is not None else 0)
    if before is not None:
        (square_ref,) = take(1)
        first = 256 * CHUNKS[before][0]
        total = own_ref[...]
        for ref in got:
            total = total + ref[:, pl.ds(skip, width)].astype(F32)
        for block in range(4):
            rows = slice(BLK * block, BLK * block + BLK)
            kept = (total[rows] * ms_ref[pl.ds(block, 1), pl.ds(first, width)]).astype(BF)
            square_ref[rows, :] = kept
            for out in outs:
                out[rows, pl.ds(0, width)] = kept
    if now is not None:
        partial_ref, right = take(2)
        load_pieces(pieces, mt_ref, 8 * CHUNKS[now][0], right)
        for start in range(0, right.shape[0], 256):
            block = dot(left_ref[...], right[pl.ds(start, 256), :], NT)
            partial_ref[:, pl.ds(start, 256)] = block[:128]
            for quarter in range(3):
                rows = 128 * (quarter + 1)
                outs[quarter][:, pl.ds(width + start, 256)] = block[rows : rows + 128].astype(BF)


def product_two_kernel(chunks, n_pieces, first, last, s_ref, mk_ref, mc_ref, *refs):
    z, core, col, layer = s_ref[0], s_ref[1], s_ref[2], s_ref[3]
    refs = list(refs)
    total = refs.pop() if last else None
    right, square = refs[-2:]
    before = None if first else refs.pop(0)
    squares, refs = refs[: 4 * len(chunks)], refs[4 * len(chunks) :]
    pieces, outs = refs[:n_pieces], refs[n_pieces:-2]
    slots = [slot for chunk in chunks for slot in CHUNKS[chunk]]
    load_pieces(pieces, mk_ref, 8 * slots[0], right)
    start = 0
    for n in range(len(chunks)):
        width = squares[4 * n].shape[1]
        for quarter in range(4):
            square[pl.ds(128 * quarter, 128), pl.ds(start, width)] = squares[4 * n + quarter][...]
        start += width
    if not last:
        total = outs[0]
    for cols in range(0, 2048, 256):
        block = dot(square[...], right[:, pl.ds(cols, 256)])
        for row in range(16):
            rows = slice(BLK * row, BLK * row + BLK)
            part = block[rows] * mc_ref[pl.ds(row, 1), pl.ds(cols, 256)]
            if not first:
                part = part + before[rows, pl.ds(cols, 256)]
            total[rows, pl.ds(cols, 256)] = part
    for n, slot in enumerate(slots):
        chip = lax.rem(z + SLOTS[slot] + 8, 8)

        @pl.when(chip // 2 == col)
        def _():
            for other in range(2):
                band = 2 * chip + lax.rem(core + other, 2) - 4 * col
                cols = pl.ds(pl.multiple_of(512 * band + 128 * layer, 128), 128)
                total[:, cols] += 3.0 * square[:, pl.ds(256 * n + 128 * other, 128)].astype(F32)

    if last:
        for share in range(4):
            cols = pl.ds(pl.multiple_of(512 * lax.rem(layer + share, 4), 512), 512)
            outs[share][...] = total[:, cols].astype(outs[share].dtype)


def finish_kernel(s_ref, own_ref, a_ref, b_ref, c_ref, out_ref):
    col = s_ref[2]
    for quarter in range(4):
        rows = slice(128 * quarter, 128 * quarter + 128)
        total = own_ref[rows] + a_ref[rows].astype(F32) + b_ref[rows].astype(F32) + c_ref[rows].astype(F32)
        out_ref[pl.ds(pl.multiple_of(128 * lax.rem(col + quarter, 4), 128), 128), :] = total.astype(BF)


def shift(array, axis, step, size):
    return lax.ppermute(array, axis, [(i, (i + step) % size) for i in range(size)])


def swap(array):
    return lax.ppermute(array, "row", [(i, i ^ 1) for i in range(16)])


def exchange(parts, axis):
    got = [shift(part, axis, step, 4) for part, step in zip(parts, (1, 2, 3))]
    return got[2], got[1], got[0]


def gather_patterns(pattern_density, pattern_square):
    rows = pattern_density.astype(BF)
    pairs = [(row, layer) for row in range(16) for layer in range(4)]
    rows = [
        lax.ppermute(
            rows,
            ("row", "rep"),
            [(4 * row + layer, 4 * ((row - 2 * (layer + far)) % 16) + layer) for row, layer in pairs],
        )
        for far in (0, 4)
    ]
    rows = jnp.concatenate(rows, 0)
    rows = jnp.concatenate([rows, swap(rows)], 0)
    rows = jnp.concatenate([rows, *exchange([rows] * 3, "rep"), pattern_square.astype(BF)], 0)
    return [rows, *exchange([rows] * 3, "col")]


def body(density, pattern_density, pattern_square, pattern_cube):
    row, col, layer = lax.axis_index("row"), lax.axis_index("col"), lax.axis_index("rep")
    where = jnp.stack([row // 2, row % 2, col, layer]).astype(jnp.int32)
    own = lax.dynamic_slice_in_dim(density, 128 * layer, 128, 0)

    up, down = [own], [own]
    for step in range(1, 5):
        first, second = up[-1], down[-1]
        if step == 4:
            first, second = first[:64], second[64:]
        up.append(shift(first, "row", 2, 16))
        down.append(shift(second, "row", -2, 16))
    held = {0: [own], 4: [up[4], down[4]]}
    for step in (1, 2, 3):
        held[-step], held[step] = [up[step]], [down[step]]
    pieces = []
    for offset in SLOTS:
        pieces.append(held[offset] + [swap(piece) for piece in held[offset]])

    both = gather_patterns(pattern_density, pattern_square)
    left, mk, mt, ms, mc = call(
        prep_kernel,
        (
            shape(512, 2048),
            shape(64, 2048, dtype=F32),
            shape(64, 2048, dtype=F32),
            shape(16, 2048, dtype=F32),
            shape(16, 2048, dtype=F32),
        ),
        8,
        flops=2 * 200 * 256 * 2048,
        byts=6 << 20,
    )(where, *both, pattern_density, pattern_cube, density)

    squares = []
    for number, slots in enumerate(CHUNKS):
        width = 256 * len(slots)
        held = [piece for slot in slots for piece in pieces[slot]]
        *others, mine = call(
            functools.partial(stage_kernel, None, number, len(held)),
            (shape(128, width),) * 3 + (shape(128, width, dtype=F32),),
            3 + len(held),
            [pltpu.VMEM((width, 2048), BF)],
            flops=2 * 512 * 2048 * width,
            byts=2 * 2048 * (512 + width),
        )(where, left, mt, *held)
        got = exchange(others, "col")
        (mine,) = call(
            functools.partial(stage_kernel, number, None, 0),
            (shape(128, width),),
            6,
            byts=2 * 128 * width * 6,
        )(where, ms, mine, *got)
        squares.append((mine, *exchange([mine] * 3, "col")))

    total = []
    for number, chunks in enumerate(PHASES):
        first, last = number == 0, number == len(PHASES) - 1
        held = [piece for chunk in chunks for slot in CHUNKS[chunk] for piece in pieces[slot]]
        blocks = [block for chunk in chunks for block in squares[chunk]]
        width = sum(squares[chunk][0].shape[1] for chunk in chunks)
        scratch = [pltpu.VMEM((width, 2048), BF), pltpu.VMEM((512, width), BF)]
        if last:
            out = (shape(512, 512, dtype=F32), shape(512, 512), shape(512, 512), shape(512, 512))
            scratch.append(pltpu.VMEM((512, 2048), F32))
        else:
            out = (shape(512, 2048, dtype=F32),)
        total = call(
            functools.partial(product_two_kernel, chunks, len(held), first, last),
            out,
            3 + len(total) + len(blocks) + len(held),
            scratch,
            flops=2 * 512 * 2048 * width,
            byts=2 * 2048 * (1024 + width),
            aliases={} if first or last else {3: 0},
        )(where, mk, mc, *total, *blocks, *held)
    mine, *others = total
    return call(finish_kernel, shape(512, 512), 5, byts=3 << 20)(where, mine, *exchange(others, "rep"))


def solution(mesh):
    placed = (P("row", "col"), P("row", "col"), P("row", "col"), P("row", "col"))
    return jax.shard_map(
        body, mesh=mesh, in_specs=placed, out_specs=P("row", ("col", "rep")), check_vma=False
    )
```

```python
import functools

import jax
import jax.numpy as jnp
from jax import lax
from jax.experimental import pallas as pl
from jax.experimental.pallas import tpu as pltpu
from jax.sharding import PartitionSpec as P

BLK = 32
BF = jnp.bfloat16
F32 = jnp.float32
VMEM = pl.BlockSpec(memory_space=pltpu.VMEM)
SMEM = pl.BlockSpec(memory_space=pltpu.SMEM)
NT = (((1,), (1,)), ((), ()))
NN = (((1,), (0,)), ((), ()))

SLOTS = (0, -1, 1, -2, 2, -3, 3, 4)
CHUNKS = ((0, 1, 2), (3, 4), (5, 6), (7,))
PHASES = ((0, 1), (2,), (3,))


def call(kernel, out_shape, n_in, scratch=(), flops=0, byts=0, mib=24, aliases={}):
    return pl.pallas_call(
        kernel,
        out_shape=out_shape,
        in_specs=[SMEM] + [VMEM] * (n_in - 1),
        out_specs=jax.tree.map(lambda _: VMEM, out_shape),
        scratch_shapes=list(scratch),
        input_output_aliases=aliases,
        compiler_params=pltpu.CompilerParams(vmem_limit_bytes=mib << 20),
        cost_estimate=pl.CostEstimate(flops=flops, bytes_accessed=byts, transcendentals=0),
    )


def shape(*dims, dtype=BF):
    return jax.ShapeDtypeStruct(dims, dtype)


def iota(dims, axis):
    return lax.broadcasted_iota(jnp.int32, dims, axis)


def dot(a, b, dims=NN):
    return lax.dot_general(a, b, dims, preferred_element_type=F32)


def row_of_slot(index, z, core, layer):
    slot = index // 8
    other = (index // 4) % 2
    offset = jnp.where(slot == 7, 4, jnp.where(slot % 2 == 1, -((slot + 1) // 2), slot // 2))
    chip = lax.rem(z + offset + 8, 8)
    band = 2 * chip + lax.rem(core + other, 2)
    return 16 * band + 4 * layer + index % 4


def prep_kernel(s_ref, *refs):
    both_ref, local_ref, cube_ref, density_ref, left_ref, mk_ref, mt_ref, ms_ref, mc_ref = refs
    z, core, col, layer = s_ref[0], s_ref[1], s_ref[2], s_ref[3]
    wide = (iota((64, 2048), 0) == iota((64, 2048), 1) // BLK).astype(BF)
    roll = (iota((16, 16), 1) == lax.rem(iota((16, 16), 0) + 4 * col, 16)).astype(BF)
    local = dot(dot(roll, local_ref[...].astype(BF)).astype(BF), wide).astype(BF)
    for quarter in range(4):
        start = pl.multiple_of(128 * lax.rem(col + quarter, 4), 128)
        for block in range(4):
            at = 4 * quarter + block
            left_ref[pl.ds(BLK * at, BLK), :] = (
                density_ref[pl.ds(start + BLK * block, BLK), :] * local[at : at + 1, :]
            )
    at = iota((64, 1024), 1)
    block_row = 16 * (at // 64) + at % 16
    mine_too = (at // 16) % 4
    share = row_of_slot(iota((64, 1024), 0), z, core, layer)
    pick = jnp.where((block_row == share) & (mine_too == col), 1.0, 0.0).astype(BF)
    both = both_ref[...].reshape(1024, 128)
    mk = dot(pick, both)[:, :64].astype(BF)
    mt = jnp.zeros((64, 64), F32)
    ms = jnp.zeros((16, 64), F32)
    square_row = iota((16, 1024), 0) + 16 * (2 * z + core)
    square_at = iota((16, 1024), 1)
    square_block = 16 * (square_at // 64) + square_at % 16
    for n in range(4):
        mine = (block_row == 64 * col + iota((64, 1024), 0)) & (mine_too == n)
        rows = dot(jnp.where(mine, 1.0, 0.0).astype(BF), both)[:, :64].astype(BF)
        column = 64 * n + iota((64, 64), 1)
        take = (column == row_of_slot(iota((64, 64), 0), z, core, layer)).astype(BF)
        mt = mt + dot(take, rows, NT)
        own = (square_block == square_row) & ((square_at // 16) % 4 == n)
        rows = dot(jnp.where(own, 1.0, 0.0).astype(BF), both)[:, 64:].astype(BF)
        ms = ms + dot(dot(roll, rows).astype(BF), take, NT)
    mk_ref[...] = dot(mk, wide)
    mt_ref[...] = dot(mt.astype(BF), wide)
    ms_ref[...] = dot(ms.astype(BF), wide)
    mc_ref[...] = -2.0 * dot(dot(roll, cube_ref[...].astype(BF)).astype(BF), wide)


def load_pieces(piece_refs, mask_ref, block_row, out_ref):
    done = 0
    for ref in piece_refs:
        for block in range(ref.shape[0] // BLK):
            row = block_row + done // BLK
            keep = jnp.broadcast_to(mask_ref[pl.ds(row, 1), :], (BLK, 2048)).astype(BF)
            out_ref[pl.ds(done, BLK), :] = ref[pl.ds(BLK * block, BLK), :] * keep
            done += BLK


def product_one_kernel(slots, n_pieces, s_ref, left_ref, mt_ref, *refs):
    col = s_ref[2]
    pieces, (send_ref, own_ref, right) = refs[:n_pieces], refs[n_pieces:]
    load_pieces(pieces, mt_ref, 8 * slots[0], right)
    for start in range(0, right.shape[0], 256):
        block = dot(left_ref[...], right[pl.ds(start, 256), :], NT)
        own_ref[:, pl.ds(start, 256)] = block[:128]
        for quarter in range(4):
            rows = slice(128 * quarter, 128 * quarter + 128)
            send_ref[lax.rem(col + quarter, 4), :, pl.ds(start, 256)] = block[rows].astype(BF)


def square_kernel(slots, s_ref, ms_ref, own_ref, got_ref, out_ref):
    col = s_ref[2]
    total = own_ref[...]
    for quarter in range(1, 4):
        total = total + got_ref[lax.rem(col + quarter, 4)].astype(F32)
    for block in range(4):
        rows = slice(BLK * block, BLK * block + BLK)
        keep = ms_ref[pl.ds(block, 1), pl.ds(256 * slots[0], total.shape[1])]
        kept = (total[rows] * keep).astype(BF)
        for quarter in range(4):
            out_ref[quarter, rows, :] = kept


def product_two_kernel(chunks, n_pieces, first, last, s_ref, mk_ref, mc_ref, *refs):
    z, core, col, layer = s_ref[0], s_ref[1], s_ref[2], s_ref[3]
    refs = list(refs)
    total = refs.pop() if last else None
    right, square = refs[-2:]
    before = None if first else refs.pop(0)
    squares, refs = refs[: len(chunks)], refs[len(chunks) :]
    pieces, outs = refs[:n_pieces], refs[n_pieces:-2]
    slots = [slot for chunk in chunks for slot in CHUNKS[chunk]]
    load_pieces(pieces, mk_ref, 8 * slots[0], right)
    start = 0
    for n in range(len(chunks)):
        width = squares[n].shape[2]
        for quarter in range(4):
            square[pl.ds(128 * quarter, 128), pl.ds(start, width)] = squares[n][lax.rem(col + quarter, 4)]
        start += width
    if not last:
        total = outs[0]
    for cols in range(0, 2048, 256):
        block = dot(square[...], right[:, pl.ds(cols, 256)])
        for row in range(16):
            rows = slice(BLK * row, BLK * row + BLK)
            part = block[rows] * mc_ref[pl.ds(row, 1), pl.ds(cols, 256)]
            if not first:
                part = part + before[rows, pl.ds(cols, 256)]
            total[rows, pl.ds(cols, 256)] = part
    for n, slot in enumerate(slots):
        chip = lax.rem(z + SLOTS[slot] + 8, 8)

        @pl.when(chip // 2 == col)
        def _():
            for other in range(2):
                band = 2 * chip + lax.rem(core + other, 2) - 4 * col
                cols = pl.ds(pl.multiple_of(512 * band + 128 * layer, 128), 128)
                total[:, cols] += 3.0 * square[:, pl.ds(256 * n + 128 * other, 128)].astype(F32)

    if last:
        for share in range(4):
            outs[0][share] = total[:, pl.ds(512 * share, 512)].astype(BF)
        outs[1][...] = total[:, pl.ds(pl.multiple_of(512 * layer, 512), 512)]


def finish_kernel(s_ref, own_ref, got_ref, out_ref):
    col, layer = s_ref[2], s_ref[3]
    for quarter in range(4):
        rows = pl.ds(128 * quarter, 128)
        total = own_ref[rows, :]
        for share in range(1, 4):
            total = total + got_ref[lax.rem(layer + share, 4), rows, :].astype(F32)
        out_ref[pl.ds(pl.multiple_of(128 * lax.rem(col + quarter, 4), 128), 128), :] = total.astype(BF)


def shift(array, axis, step, size):
    return lax.ppermute(array, axis, [(i, (i + step) % size) for i in range(size)])


def swap(array):
    return lax.ppermute(array, "row", [(i, i ^ 1) for i in range(16)])


def exchange(parts, axis):
    return lax.all_to_all(parts, axis, 0, 0)


def gather_patterns(pattern_density, pattern_square):
    both = jnp.concatenate([pattern_density, pattern_square], 1).astype(BF)
    return exchange(jnp.broadcast_to(both, (64, 16, 128)), ("row", "col"))


def body(density, pattern_density, pattern_square, pattern_cube):
    row, col, layer = lax.axis_index("row"), lax.axis_index("col"), lax.axis_index("rep")
    where = jnp.stack([row // 2, row % 2, col, layer]).astype(jnp.int32)
    own = lax.dynamic_slice_in_dim(density, 128 * layer, 128, 0)

    up, down = [own], [own]
    for step in range(1, 5):
        first, second = up[-1], down[-1]
        if step == 4:
            first, second = first[:64], second[64:]
        up.append(shift(first, "row", 2, 16))
        down.append(shift(second, "row", -2, 16))
    held = {0: [own], 4: [up[4], down[4]]}
    for step in (1, 2, 3):
        held[-step], held[step] = [up[step]], [down[step]]
    pieces = []
    for offset in SLOTS:
        pieces.append(held[offset] + [swap(piece) for piece in held[offset]])

    both = gather_patterns(pattern_density, pattern_square)
    left, mk, mt, ms, mc = call(
        prep_kernel,
        (
            shape(512, 2048),
            shape(64, 2048, dtype=F32),
            shape(64, 2048, dtype=F32),
            shape(16, 2048, dtype=F32),
            shape(16, 2048, dtype=F32),
        ),
        5,
        flops=2 * 200 * 256 * 2048,
        byts=6 << 20,
    )(where, both, pattern_density, pattern_cube, density)

    squares = []
    for number, slots in enumerate(CHUNKS):
        width = 256 * len(slots)
        held = [piece for slot in slots for piece in pieces[slot]]
        send, mine = call(
            functools.partial(product_one_kernel, slots, len(held)),
            (shape(4, 128, width), shape(128, width, dtype=F32)),
            3 + len(held),
            [pltpu.VMEM((width, 2048), BF)],
            flops=2 * 512 * 2048 * width,
            byts=2 * 2048 * (512 + width),
        )(where, left, mt, *held)
        mine = call(
            functools.partial(square_kernel, slots),
            shape(4, 128, width),
            4,
            byts=2 * 128 * width * 6,
        )(where, ms, mine, exchange(send, "col"))
        squares.append(exchange(mine, "col"))

    total = []
    for number, chunks in enumerate(PHASES):
        first, last = number == 0, number == len(PHASES) - 1
        held = [piece for chunk in chunks for slot in CHUNKS[chunk] for piece in pieces[slot]]
        blocks = [squares[chunk] for chunk in chunks]
        width = sum(block.shape[2] for block in blocks)
        scratch = [pltpu.VMEM((width, 2048), BF), pltpu.VMEM((512, width), BF)]
        if last:
            out = (shape(4, 512, 512), shape(512, 512, dtype=F32))
            scratch.append(pltpu.VMEM((512, 2048), F32))
        else:
            out = (shape(512, 2048, dtype=F32),)
        total = call(
            functools.partial(product_two_kernel, chunks, len(held), first, last),
            out,
            3 + len(total) + len(blocks) + len(held),
            scratch,
            flops=2 * 512 * 2048 * width,
            byts=2 * 2048 * (1024 + width),
            aliases={} if first or last else {3: 0},
        )(where, mk, mc, *total, *blocks, *held)
    send, mine = total
    return call(finish_kernel, shape(512, 512), 3, byts=3 << 20)(where, mine, exchange(send, "rep"))


def solution(mesh):
    placed = (P("row", "col"), P("row", "col"), P("row", "col"), P("row", "col"))
    return jax.shard_map(
        body, mesh=mesh, in_specs=placed, out_specs=P("row", ("col", "rep")), check_vma=False
    )
```

```python
import functools

import jax
import jax.numpy as jnp
from jax import lax
from jax.experimental import pallas as pl
from jax.experimental.pallas import tpu as pltpu
from jax.sharding import PartitionSpec as P

BLK = 32
BF = jnp.bfloat16
F32 = jnp.float32
VMEM = pl.BlockSpec(memory_space=pltpu.VMEM)
SMEM = pl.BlockSpec(memory_space=pltpu.SMEM)
NT = (((1,), (1,)), ((), ()))
NN = (((1,), (0,)), ((), ()))

SLOTS = (0, -1, 1, -2, 2, -3, 3, 4)
EARLY = 3
HALVES = 2


def call(kernel, out_shape, n_in, scratch=(), flops=0, byts=0, mib=24, aliases={}):
    return pl.pallas_call(
        kernel,
        out_shape=out_shape,
        in_specs=[SMEM] + [VMEM] * (n_in - 1),
        out_specs=jax.tree.map(lambda _: VMEM, out_shape),
        scratch_shapes=list(scratch),
        input_output_aliases=aliases,
        compiler_params=pltpu.CompilerParams(vmem_limit_bytes=mib << 20),
        cost_estimate=pl.CostEstimate(flops=flops, bytes_accessed=byts, transcendentals=0),
    )


def shape(*dims, dtype=BF):
    return jax.ShapeDtypeStruct(dims, dtype)


def iota(dims, axis):
    return lax.broadcasted_iota(jnp.int32, dims, axis)


def dot(a, b, dims=NN):
    return lax.dot_general(a, b, dims, preferred_element_type=F32)


def row_of_slot(index, z, core, layer):
    slot = index // 8
    other = (index // 4) % 2
    offset = jnp.where(slot == 7, 4, jnp.where(slot % 2 == 1, -((slot + 1) // 2), slot // 2))
    chip = lax.rem(z + offset + 8, 8)
    band = 2 * chip + lax.rem(core + other, 2)
    return 16 * band + 4 * layer + index % 4


def prep_kernel(s_ref, *refs):
    both_ref, local_ref, cube_ref, density_ref, left_ref, mk_ref, mt_ref, ms_ref, mc_ref = refs
    z, core, col, layer = s_ref[0], s_ref[1], s_ref[2], s_ref[3]
    wide = (iota((64, 2048), 0) == iota((64, 2048), 1) // BLK).astype(BF)
    roll = (iota((16, 16), 1) == lax.rem(iota((16, 16), 0) + 4 * col, 16)).astype(BF)
    local = dot(dot(roll, local_ref[...].astype(BF)).astype(BF), wide).astype(BF)
    for quarter in range(4):
        start = pl.multiple_of(128 * lax.rem(col + quarter, 4), 128)
        for block in range(4):
            at = 4 * quarter + block
            left_ref[pl.ds(BLK * at, BLK), :] = (
                density_ref[pl.ds(start + BLK * block, BLK), :] * local[at : at + 1, :]
            )
    at = iota((64, 1024), 1)
    block_row = 16 * (at // 64) + at % 16
    mine_too = (at // 16) % 4
    share = row_of_slot(iota((64, 1024), 0), z, core, layer)
    pick = jnp.where((block_row == share) & (mine_too == col), 1.0, 0.0).astype(BF)
    both = both_ref[...].reshape(1024, 128)
    mk = dot(pick, both)[:, :64].astype(BF)
    mt = jnp.zeros((64, 64), F32)
    ms = jnp.zeros((16, 64), F32)
    square_row = iota((16, 1024), 0) + 16 * (2 * z + core)
    square_at = iota((16, 1024), 1)
    square_block = 16 * (square_at // 64) + square_at % 16
    for n in range(4):
        mine = (block_row == 64 * col + iota((64, 1024), 0)) & (mine_too == n)
        rows = dot(jnp.where(mine, 1.0, 0.0).astype(BF), both)[:, :64].astype(BF)
        column = 64 * n + iota((64, 64), 1)
        take = (column == row_of_slot(iota((64, 64), 0), z, core, layer)).astype(BF)
        mt = mt + dot(take, rows, NT)
        own = (square_block == square_row) & ((square_at // 16) % 4 == n)
        rows = dot(jnp.where(own, 1.0, 0.0).astype(BF), both)[:, 64:].astype(BF)
        ms = ms + dot(dot(roll, rows).astype(BF), take, NT)
    mk_ref[...] = dot(mk, wide)
    mt_ref[...] = dot(mt.astype(BF), wide)
    ms_ref[...] = dot(ms.astype(BF), wide)
    mc_ref[...] = -2.0 * dot(dot(roll, cube_ref[...].astype(BF)).astype(BF), wide)


def load_pieces(piece_refs, mask_ref, block_row, out_ref):
    done = 0
    for ref in piece_refs:
        for block in range(ref.shape[0] // BLK):
            row = block_row + done // BLK
            keep = jnp.broadcast_to(mask_ref[pl.ds(row, 1), :], (BLK, 2048)).astype(BF)
            out_ref[pl.ds(done, BLK), :] = ref[pl.ds(BLK * block, BLK), :] * keep
            done += BLK


def load_slots(slots, where, gathered_ref, mask_ref, out_ref):
    z, core = where
    for n, slot in enumerate(slots):
        chip = lax.rem(z + SLOTS[slot] + 8, 8)
        for other in range(2):
            start = pl.multiple_of(128 * (2 * chip + lax.rem(core + other, 2)), 128)
            for block in range(4):
                row = 8 * slot + 4 * other + block
                keep = jnp.broadcast_to(mask_ref[pl.ds(row, 1), :], (BLK, 2048)).astype(BF)
                out_ref[pl.ds(256 * n + 128 * other + BLK * block, BLK), :] = (
                    gathered_ref[pl.ds(start + BLK * block, BLK), :] * keep
                )


def product_one_kernel(slots, halves, n_pieces, s_ref, left_ref, mt_ref, *refs):
    pieces, outs, right = refs[:n_pieces], refs[n_pieces:-1], refs[-1]
    if n_pieces > 1:
        load_pieces(pieces, mt_ref, 8 * slots[0], right)
    else:
        load_slots(slots, (s_ref[0], s_ref[1]), pieces[0], mt_ref, right)
    height = 128 // halves
    for start in range(0, right.shape[0], 256):
        block = dot(left_ref[...], right[pl.ds(start, 256), :], NT)
        for half in range(halves):
            for quarter in range(4):
                row = 128 * quarter + height * half
                out = outs[4 * half + quarter]
                out[:, pl.ds(start, 256)] = block[row : row + height].astype(out.dtype)


def square_kernel(first_slot, first_block, s_ref, ms_ref, own_ref, a_ref, b_ref, c_ref, out_ref):
    height, width = out_ref.shape
    total = own_ref[...] + a_ref[...].astype(F32) + b_ref[...].astype(F32) + c_ref[...].astype(F32)
    for block in range(height // BLK):
        rows = slice(BLK * block, BLK * block + BLK)
        keep = ms_ref[pl.ds(first_block + block, 1), pl.ds(256 * first_slot, width)]
        out_ref[rows, :] = (total[rows] * keep).astype(BF)


def right_kernel(s_ref, mk_ref, gathered_ref, out_ref):
    load_slots(range(len(SLOTS)), (s_ref[0], s_ref[1]), gathered_ref, mk_ref, out_ref)


def product_two_kernel(half, n_early, s_ref, mc_ref, right_ref, *refs):
    z, core, col, layer = s_ref[0], s_ref[1], s_ref[2], s_ref[3]
    early, late, outs = refs[:n_early], refs[n_early : n_early + 4], refs[n_early + 4 : n_early + 8]
    square, total = refs[-2:]
    height = 128 // HALVES
    skip = 256 * EARLY if n_early else 0
    for quarter in range(4):
        rows = pl.ds(height * quarter, height)
        if n_early:
            square[rows, pl.ds(0, skip)] = early[quarter][pl.ds(height * half, height), :]
        square[rows, pl.ds(skip, 2048 - skip)] = late[quarter][...]
    for cols in range(0, 2048, 256):
        block = dot(square[...], right_ref[:, pl.ds(cols, 256)])
        for n in range(4 * height // BLK):
            row = 4 * (n // (height // BLK)) + height // BLK * half + n % (height // BLK)
            rows = slice(BLK * n, BLK * n + BLK)
            total[rows, pl.ds(cols, 256)] = block[rows] * mc_ref[pl.ds(row, 1), pl.ds(cols, 256)]
    for slot in range(len(SLOTS)):
        chip = lax.rem(z + SLOTS[slot] + 8, 8)

        @pl.when(chip // 2 == col)
        def _():
            for other in range(2):
                band = 2 * chip + lax.rem(core + other, 2) - 4 * col
                cols = pl.ds(pl.multiple_of(512 * band + 128 * layer, 128), 128)
                total[:, cols] += 3.0 * square[:, pl.ds(256 * slot + 128 * other, 128)].astype(F32)

    for share in range(4):
        cols = pl.ds(pl.multiple_of(512 * lax.rem(layer + share, 4), 512), 512)
        outs[share][...] = total[:, cols].astype(outs[share].dtype)


def finish_kernel(s_ref, *refs):
    col, out_ref = s_ref[2], refs[-1]
    height = 128 // HALVES
    for half in range(HALVES):
        own_ref, *got = refs[4 * half : 4 * half + 4]
        for quarter in range(4):
            rows = pl.ds(height * quarter, height)
            total = own_ref[rows, :]
            for ref in got:
                total = total + ref[rows, :].astype(F32)
            start = 128 * lax.rem(col + quarter, 4) + height * half
            out_ref[pl.ds(pl.multiple_of(start, height), height), :] = total.astype(BF)


def shift(array, axis, step, size):
    return lax.ppermute(array, axis, [(i, (i + step) % size) for i in range(size)])


def swap(array):
    return lax.ppermute(array, "row", [(i, i ^ 1) for i in range(16)])


def exchange(parts, axis):
    got = [shift(part, axis, step, 4) for part, step in zip(parts, (1, 2, 3))]
    return got[2], got[1], got[0]


def gather_patterns(pattern_density, pattern_square):
    both = jnp.concatenate([pattern_density, pattern_square], 1).astype(BF)
    return lax.all_to_all(jnp.broadcast_to(both, (64, 16, 128)), ("row", "col"), 0, 0)


def body(density, pattern_density, pattern_square, pattern_cube):
    row, col, layer = lax.axis_index("row"), lax.axis_index("col"), lax.axis_index("rep")
    where = jnp.stack([row // 2, row % 2, col, layer]).astype(jnp.int32)
    own = lax.dynamic_slice_in_dim(density, 128 * layer, 128, 0)

    gathered = lax.all_gather(own, "row", axis=0, tiled=True)
    near = [own, shift(own, "row", 2, 16), shift(own, "row", -2, 16)][:EARLY]
    early = [piece for one in near for piece in (one, swap(one))]

    both = gather_patterns(pattern_density, pattern_square)
    left, mk, mt, ms, mc = call(
        prep_kernel,
        (
            shape(512, 2048),
            shape(64, 2048, dtype=F32),
            shape(64, 2048, dtype=F32),
            shape(16, 2048, dtype=F32),
            shape(16, 2048, dtype=F32),
        ),
        5,
        flops=2 * 200 * 256 * 2048,
        byts=6 << 20,
    )(where, both, pattern_density, pattern_cube, density)

    def start(slots, halves, held):
        height, width = 128 // halves, 256 * len(slots)
        parts = call(
            functools.partial(product_one_kernel, slots, halves, len(held)),
            ((shape(height, width, dtype=F32),) + (shape(height, width),) * 3) * halves,
            3 + len(held),
            [pltpu.VMEM((width, 2048), BF)],
            flops=2 * 512 * 2048 * width,
            byts=2 * 2048 * (512 + width),
        )(where, left, mt, *held)
        squares = []
        for half in range(halves):
            mine, *others = parts[4 * half : 4 * half + 4]
            mine = call(
                functools.partial(square_kernel, slots[0], half * (4 // halves)),
                shape(height, width),
                6,
                byts=2 * height * width * 6,
            )(where, ms, mine, *exchange(others, "col"))
            squares.append((mine, *exchange([mine] * 3, "col")))
        return squares

    first = start(range(EARLY), 1, early)[0] if EARLY else ()
    first, gathered = lax.optimization_barrier((first, gathered))
    squares = start(range(EARLY, len(SLOTS)), HALVES, [gathered])
    right = call(right_kernel, shape(2048, 2048), 3, byts=16 << 20)(where, mk, gathered)
    results = []
    for half in range(HALVES):
        height = 512 // HALVES
        mine, *others = call(
            functools.partial(product_two_kernel, half, len(first)),
            (shape(height, 512, dtype=F32),) + (shape(height, 512),) * 3,
            3 + len(first) + 4,
            [pltpu.VMEM((height, 2048), BF), pltpu.VMEM((height, 2048), F32)],
            flops=2 * height * 2048 * 2048,
            byts=10 << 20,
        )(where, mc, right, *first, *squares[half])
        results += [mine, *exchange(others, "rep")]
    return call(finish_kernel, shape(512, 512), 1 + len(results), byts=3 << 20)(where, *results)


def solution(mesh):
    placed = (P("row", "col"), P("row", "col"), P("row", "col"), P("row", "col"))
    return jax.shard_map(
        body, mesh=mesh, in_specs=placed, out_specs=P("row", ("col", "rep")), check_vma=False
    )
```

```python
import functools

import jax
import jax.numpy as jnp
from jax import lax
from jax.experimental import pallas as pl
from jax.experimental.pallas import tpu as pltpu
from jax.sharding import PartitionSpec as P

BLK = 32
BF = jnp.bfloat16
F32 = jnp.float32
VMEM = pl.BlockSpec(memory_space=pltpu.VMEM)
SMEM = pl.BlockSpec(memory_space=pltpu.SMEM)
NT = (((1,), (1,)), ((), ()))
NN = (((1,), (0,)), ((), ()))

SLOTS = (0, -1, 1, -2, 2, -3, 3, 4)
EARLY = 3
HALVES = 2


def call(kernel, out_shape, n_in, scratch=(), flops=0, byts=0, mib=20, aliases={}):
    return pl.pallas_call(
        kernel,
        out_shape=out_shape,
        in_specs=[SMEM] + [VMEM] * (n_in - 1),
        out_specs=jax.tree.map(lambda _: VMEM, out_shape),
        scratch_shapes=list(scratch),
        input_output_aliases=aliases,
        compiler_params=pltpu.CompilerParams(vmem_limit_bytes=mib << 20),
        cost_estimate=pl.CostEstimate(flops=flops, bytes_accessed=byts, transcendentals=0),
    )


def shape(*dims, dtype=BF):
    return jax.ShapeDtypeStruct(dims, dtype)


def iota(dims, axis):
    return lax.broadcasted_iota(jnp.int32, dims, axis)


def dot(a, b, dims=NN):
    return lax.dot_general(a, b, dims, preferred_element_type=F32)


def row_of_slot(index, z, core, layer):
    slot = index // 8
    other = (index // 4) % 2
    offset = jnp.where(slot == 7, 4, jnp.where(slot % 2 == 1, -((slot + 1) // 2), slot // 2))
    chip = lax.rem(z + offset + 8, 8)
    band = 2 * chip + lax.rem(core + other, 2)
    return 16 * band + 4 * layer + index % 4


def prep_kernel(s_ref, *refs):
    both_ref, local_ref, cube_ref, density_ref, left_ref, mk_ref, mt_ref, ms_ref, mc_ref = refs
    z, core, col, layer = s_ref[0], s_ref[1], s_ref[2], s_ref[3]
    wide = (iota((64, 2048), 0) == iota((64, 2048), 1) // BLK).astype(BF)
    roll = (iota((16, 16), 1) == lax.rem(iota((16, 16), 0) + 4 * col, 16)).astype(BF)
    local = dot(dot(roll, local_ref[...].astype(BF)).astype(BF), wide).astype(BF)
    for quarter in range(4):
        start = pl.multiple_of(128 * lax.rem(col + quarter, 4), 128)
        for block in range(4):
            at = 4 * quarter + block
            left_ref[pl.ds(BLK * at, BLK), :] = (
                density_ref[pl.ds(start + BLK * block, BLK), :] * local[at : at + 1, :]
            )
    at = iota((64, 1024), 1)
    block_row = 16 * (at // 64) + at % 16
    mine_too = (at // 16) % 4
    share = row_of_slot(iota((64, 1024), 0), z, core, layer)
    pick = jnp.where((block_row == share) & (mine_too == col), 1.0, 0.0).astype(BF)
    both = both_ref[...].reshape(1024, 128)
    mk = dot(pick, both)[:, :64].astype(BF)
    mt = jnp.zeros((64, 64), F32)
    ms = jnp.zeros((16, 64), F32)
    square_row = iota((16, 1024), 0) + 16 * (2 * z + core)
    square_at = iota((16, 1024), 1)
    square_block = 16 * (square_at // 64) + square_at % 16
    for n in range(4):
        mine = (block_row == 64 * col + iota((64, 1024), 0)) & (mine_too == n)
        rows = dot(jnp.where(mine, 1.0, 0.0).astype(BF), both)[:, :64].astype(BF)
        column = 64 * n + iota((64, 64), 1)
        take = (column == row_of_slot(iota((64, 64), 0), z, core, layer)).astype(BF)
        mt = mt + dot(take, rows, NT)
        own = (square_block == square_row) & ((square_at // 16) % 4 == n)
        rows = dot(jnp.where(own, 1.0, 0.0).astype(BF), both)[:, 64:].astype(BF)
        ms = ms + dot(dot(roll, rows).astype(BF), take, NT)
    mk_ref[...] = dot(mk, wide)
    mt_ref[...] = dot(mt.astype(BF), wide)
    ms_ref[...] = dot(ms.astype(BF), wide)
    mc_ref[...] = -2.0 * dot(dot(roll, cube_ref[...].astype(BF)).astype(BF), wide)


def loop(count, step):
    lax.fori_loop(0, count, lambda n, _: step(n), None)


def block_of(n, size):
    return pl.ds(pl.multiple_of(n * size, size), size)


def load_pieces(piece_refs, mask_ref, block_row, out_ref):
    done = 0
    for ref in piece_refs:

        def step(n, ref=ref, done=done):
            keep = mask_ref[pl.ds(block_row + done + n, 1), :]
            keep = jnp.broadcast_to(keep, (BLK, 2048)).astype(BF)
            out_ref[block_of(done + n, BLK), :] = ref[block_of(n, BLK), :] * keep

        loop(ref.shape[0] // BLK, step)
        done += ref.shape[0] // BLK


def product_one_kernel(slots, halves, n_pieces, s_ref, left_ref, mt_ref, *refs):
    pieces, outs, right = refs[:n_pieces], refs[n_pieces:-1], refs[-1]
    load_pieces(pieces, mt_ref, 8 * slots[0], right)
    height = 128 // halves

    def step(n):
        block = dot(left_ref[...], right[block_of(n, 256), :], NT)
        for half in range(halves):
            for quarter in range(4):
                row = 128 * quarter + height * half
                out = outs[4 * half + quarter]
                out[:, block_of(n, 256)] = block[row : row + height].astype(out.dtype)

    loop(right.shape[0] // 256, step)


def square_kernel(first_slot, first_block, s_ref, ms_ref, own_ref, a_ref, b_ref, c_ref, out_ref):
    height, width = out_ref.shape
    total = own_ref[...] + a_ref[...].astype(F32) + b_ref[...].astype(F32) + c_ref[...].astype(F32)
    for block in range(height // BLK):
        rows = slice(BLK * block, BLK * block + BLK)
        keep = ms_ref[pl.ds(first_block + block, 1), pl.ds(256 * first_slot, width)]
        out_ref[rows, :] = (total[rows] * keep).astype(BF)


def right_kernel(s_ref, mk_ref, *refs):
    load_pieces(refs[:-1], mk_ref, 0, refs[-1])


def product_two_kernel(half, n_early, s_ref, mc_ref, right_ref, *refs):
    z, core, col, layer = s_ref[0], s_ref[1], s_ref[2], s_ref[3]
    early, late, outs = refs[:n_early], refs[n_early : n_early + 4], refs[n_early + 4 : n_early + 8]
    square, total = refs[-2:]
    height = 128 // HALVES
    skip = 256 * EARLY if n_early else 0
    for quarter in range(4):
        rows = pl.ds(height * quarter, height)
        if n_early:
            square[rows, pl.ds(0, skip)] = early[quarter][pl.ds(height * half, height), :]
        square[rows, pl.ds(skip, 2048 - skip)] = late[quarter][...]

    def step(tile):
        block = dot(square[...], right_ref[:, block_of(tile, 256)])
        for n in range(4 * height // BLK):
            row = 4 * (n // (height // BLK)) + height // BLK * half + n % (height // BLK)
            rows = slice(BLK * n, BLK * n + BLK)
            total[rows, block_of(tile, 256)] = block[rows] * mc_ref[pl.ds(row, 1), block_of(tile, 256)]

    loop(8, step)

    def add(n):
        block_row = row_of_slot(4 * n, z, core, layer)
        band = block_row // 16 - 4 * col

        @pl.when((band >= 0) & (band < 4))
        def _():
            cols = pl.ds(pl.multiple_of(512 * band + 128 * layer, 128), 128)
            total[:, cols] += 3.0 * square[:, block_of(n, 128)].astype(F32)

    loop(16, add)
    for share in range(4):
        cols = pl.ds(pl.multiple_of(512 * lax.rem(layer + share, 4), 512), 512)
        outs[share][...] = total[:, cols].astype(outs[share].dtype)


def finish_kernel(s_ref, *refs):
    col, out_ref = s_ref[2], refs[-1]
    height = 128 // HALVES
    for half in range(HALVES):
        own_ref, *got = refs[4 * half : 4 * half + 4]
        for quarter in range(4):
            rows = pl.ds(height * quarter, height)
            total = own_ref[rows, :]
            for ref in got:
                total = total + ref[rows, :].astype(F32)
            start = 128 * lax.rem(col + quarter, 4) + height * half
            out_ref[pl.ds(pl.multiple_of(start, height), height), :] = total.astype(BF)


def shift(array, axis, step, size):
    return lax.ppermute(array, axis, [(i, (i + step) % size) for i in range(size)])


def swap(array):
    return lax.ppermute(array, "row", [(i, i ^ 1) for i in range(16)])


def exchange(parts, axis):
    got = [shift(part, axis, step, 4) for part, step in zip(parts, (1, 2, 3))]
    return got[2], got[1], got[0]


def body(density, pattern_density, pattern_square, pattern_cube):
    row, col, layer = lax.axis_index("row"), lax.axis_index("col"), lax.axis_index("rep")
    where = jnp.stack([row // 2, row % 2, col, layer]).astype(jnp.int32)
    own = lax.dynamic_slice_in_dim(density, 128 * layer, 128, 0)

    both = jnp.concatenate([pattern_density, pattern_square], 1).astype(BF)
    own, both = lax.optimization_barrier((own, jnp.broadcast_to(both, (64, 16, 128))))
    both = lax.all_to_all(both, ("row", "col"), 0, 0)

    def both_ways(up, down):
        return shift(up, "row", 2, 16), shift(down, "row", -2, 16)

    def with_swapped(held):
        return [*held, *(swap(piece) for piece in held)]

    first = both_ways(own, own)
    *first, both = lax.optimization_barrier((*first, both))
    second = both_ways(*first)
    left, mk, mt, ms, mc = call(
        prep_kernel,
        (
            shape(512, 2048),
            shape(64, 2048, dtype=F32),
            shape(64, 2048, dtype=F32),
            shape(16, 2048, dtype=F32),
            shape(16, 2048, dtype=F32),
        ),
        5,
        flops=2 * 200 * 256 * 2048,
        byts=6 << 20,
    )(where, both, pattern_density, pattern_cube, density)

    def multiply(slots, halves, held):
        height, width = 128 // halves, 256 * len(slots)
        return call(
            functools.partial(product_one_kernel, slots, halves, len(held)),
            ((shape(height, width, dtype=F32),) + (shape(height, width),) * 3) * halves,
            3 + len(held),
            [pltpu.VMEM((width, 2048), BF)],
            flops=2 * 512 * 2048 * width,
            byts=2 * 2048 * (512 + width),
        )(where, left, mt, *held)

    def finish_square(slots, halves, half, mine, got):
        height, width = 128 // halves, 256 * len(slots)
        mine = call(
            functools.partial(square_kernel, slots[0], half * (4 // halves)),
            shape(height, width),
            6,
            byts=2 * height * width * 6,
        )(where, ms, mine, *got)
        return mine, *exchange([mine] * 3, "col")

    early = [piece for held in ([own], first[:1], first[1:]) for piece in with_swapped(held)]
    parts = multiply(range(EARLY), 1, early)
    *second, parts = lax.optimization_barrier((*second, parts))
    third = both_ways(*second)
    third, ends, got, second = lax.optimization_barrier(
        (third, (third[0][:64], third[1][64:]), exchange(parts[1:], "col"), second)
    )
    fourth = both_ways(*ends)
    late = [with_swapped(held) for held in (second[:1], second[1:])]
    late, got = lax.optimization_barrier((late, got))
    early_square = finish_square(range(EARLY), 1, 0, parts[0], got)
    fourth, early_square = lax.optimization_barrier((fourth, early_square))
    late += [with_swapped(held) for held in (third[:1], third[1:], fourth)]
    late = [piece for held in late for piece in held]
    slots = range(EARLY, len(SLOTS))
    parts = multiply(slots, HALVES, late)
    parts = [parts[4 * half : 4 * half + 4] for half in range(HALVES)]
    squares = [
        finish_square(slots, HALVES, half, mine, exchange(others, "col")) for half, (mine, *others) in enumerate(parts)
    ]
    right = call(right_kernel, shape(2048, 2048), 2 + len(early + late), byts=16 << 20)(where, mk, *early, *late)
    results = []
    for half in range(HALVES):
        height = 512 // HALVES
        mine, *others = call(
            functools.partial(product_two_kernel, half, len(early_square)),
            (shape(height, 512, dtype=F32),) + (shape(height, 512),) * 3,
            3 + len(early_square) + 4,
            [pltpu.VMEM((height, 2048), BF), pltpu.VMEM((height, 2048), F32)],
            flops=2 * height * 2048 * 2048,
            byts=10 << 20,
        )(where, mc, right, *early_square, *squares[half])
        results += [mine, *exchange(others, "rep")]
    return call(finish_kernel, shape(512, 512), 1 + len(results), byts=3 << 20)(where, *results)


def solution(mesh):
    placed = (P("row", "col"), P("row", "col"), P("row", "col"), P("row", "col"))
    return jax.shard_map(
        body, mesh=mesh, in_specs=placed, out_specs=P("row", ("col", "rep")), check_vma=False
    )
```

```python
import functools

import jax
import jax.numpy as jnp
from jax import lax
from jax.experimental import pallas as pl
from jax.experimental.pallas import tpu as pltpu
from jax.sharding import PartitionSpec as P

BLK = 32
BF = jnp.bfloat16
F32 = jnp.float32
VMEM = pl.BlockSpec(memory_space=pltpu.VMEM)
SMEM = pl.BlockSpec(memory_space=pltpu.SMEM)
NT = (((1,), (1,)), ((), ()))
NN = (((1,), (0,)), ((), ()))

SLOTS = (0, -1, 1, -2, 2, -3, 3, 4)
EARLY = 3
HALVES = 2


def call(kernel, out_shape, n_in, scratch=(), flops=0, byts=0, mib=20, aliases={}):
    return pl.pallas_call(
        kernel,
        out_shape=out_shape,
        in_specs=[SMEM] + [VMEM] * (n_in - 1),
        out_specs=jax.tree.map(lambda _: VMEM, out_shape),
        scratch_shapes=list(scratch),
        input_output_aliases=aliases,
        compiler_params=pltpu.CompilerParams(vmem_limit_bytes=mib << 20),
        cost_estimate=pl.CostEstimate(flops=flops, bytes_accessed=byts, transcendentals=0),
    )


def shape(*dims, dtype=BF):
    return jax.ShapeDtypeStruct(dims, dtype)


def iota(dims, axis):
    return lax.broadcasted_iota(jnp.int32, dims, axis)


def dot(a, b, dims=NN):
    return lax.dot_general(a, b, dims, preferred_element_type=F32)


def row_of_slot(index, z, core, layer):
    slot = index // 8
    other = (index // 4) % 2
    offset = jnp.where(slot == 7, 4, jnp.where(slot % 2 == 1, -((slot + 1) // 2), slot // 2))
    chip = lax.rem(z + offset + 8, 8)
    band = 2 * chip + lax.rem(core + other, 2)
    return 16 * band + 4 * layer + index % 4


def prep_kernel(s_ref, *refs):
    both_ref, local_ref, cube_ref, density_ref, left_ref, mk_ref, mt_ref, ms_ref, mc_ref = refs
    z, core, col, layer = s_ref[0], s_ref[1], s_ref[2], s_ref[3]
    wide = (iota((64, 2048), 0) == iota((64, 2048), 1) // BLK).astype(BF)
    roll = (iota((16, 16), 1) == lax.rem(iota((16, 16), 0) + 4 * col, 16)).astype(BF)
    local = dot(dot(roll, local_ref[...].astype(BF)).astype(BF), wide).astype(BF)
    for quarter in range(4):
        start = pl.multiple_of(128 * lax.rem(col + quarter, 4), 128)
        for block in range(4):
            at = 4 * quarter + block
            left_ref[pl.ds(BLK * at, BLK), :] = (
                density_ref[pl.ds(start + BLK * block, BLK), :] * local[at : at + 1, :]
            )
    at = iota((64, 1280), 1)
    device, inner = at // 80, at % 80
    chip = lax.rem(z + device % 4 + 4 * ((inner // 16) % 2), 8)
    block_row = 16 * (2 * chip + lax.rem(core + inner // 32, 2)) + inner % 16
    density = inner < 64
    both = both_ref[...].reshape(1280, 64)
    pick = density & (block_row == row_of_slot(iota((64, 1280), 0), z, core, layer)) & (device // 4 == col)
    mk = dot(jnp.where(pick, 1.0, 0.0).astype(BF), both).astype(BF)
    mt = jnp.zeros((64, 64), F32)
    ms = jnp.zeros((16, 64), F32)
    order = lax.rem(iota((16, 1280), 0) + 4 * col, 16)
    square_at = iota((16, 1280), 1)
    for n in range(4):
        mine = density & (block_row == 64 * col + iota((64, 1280), 0)) & (device // 4 == n)
        rows = dot(jnp.where(mine, 1.0, 0.0).astype(BF), both).astype(BF)
        column = 64 * n + iota((64, 64), 1)
        take = (column == row_of_slot(iota((64, 64), 0), z, core, layer)).astype(BF)
        mt = mt + dot(take, rows, NT)
        own = square_at == 80 * (4 * n + layer) + 64 + order
        rows = dot(jnp.where(own, 1.0, 0.0).astype(BF), both).astype(BF)
        ms = ms + dot(rows, take, NT)
    mk_ref[...] = dot(mk, wide)
    mt_ref[...] = dot(mt.astype(BF), wide)
    ms_ref[...] = dot(ms.astype(BF), wide)
    mc_ref[...] = -2.0 * dot(dot(roll, cube_ref[...].astype(BF)).astype(BF), wide)


def load_pieces(piece_refs, mask_ref, block_row, out_ref):
    done = 0
    for ref in piece_refs:
        for block in range(ref.shape[0] // BLK):
            row = block_row + done // BLK
            keep = jnp.broadcast_to(mask_ref[pl.ds(row, 1), :], (BLK, 2048)).astype(BF)
            out_ref[pl.ds(done, BLK), :] = ref[pl.ds(BLK * block, BLK), :] * keep
            done += BLK


def product_one_kernel(slots, halves, n_pieces, s_ref, left_ref, mt_ref, *refs):
    pieces, outs, right = refs[:n_pieces], refs[n_pieces:-1], refs[-1]
    load_pieces(pieces, mt_ref, 8 * slots[0], right)
    height = 128 // halves
    for start in range(0, right.shape[0], 256):
        block = dot(left_ref[...], right[pl.ds(start, 256), :], NT)
        for half in range(halves):
            for quarter in range(4):
                row = 128 * quarter + height * half
                out = outs[4 * half + quarter]
                out[:, pl.ds(start, 256)] = block[row : row + height].astype(out.dtype)


def square_kernel(first_slot, first_block, s_ref, ms_ref, own_ref, a_ref, b_ref, c_ref, out_ref):
    height, width = out_ref.shape
    total = own_ref[...] + a_ref[...].astype(F32) + b_ref[...].astype(F32) + c_ref[...].astype(F32)
    for block in range(height // BLK):
        rows = slice(BLK * block, BLK * block + BLK)
        keep = ms_ref[pl.ds(first_block + block, 1), pl.ds(256 * first_slot, width)]
        out_ref[rows, :] = (total[rows] * keep).astype(BF)


def right_kernel(s_ref, mk_ref, *refs):
    load_pieces(refs[:-1], mk_ref, 0, refs[-1])


def product_two_kernel(half, n_early, s_ref, mc_ref, right_ref, *refs):
    z, core, col, layer = s_ref[0], s_ref[1], s_ref[2], s_ref[3]
    early, late, outs = refs[:n_early], refs[n_early : n_early + 4], refs[n_early + 4 : n_early + 8]
    square, total = refs[-2:]
    height = 128 // HALVES
    skip = 256 * EARLY if n_early else 0
    for quarter in range(4):
        rows = pl.ds(height * quarter, height)
        if n_early:
            square[rows, pl.ds(0, skip)] = early[quarter][pl.ds(height * half, height), :]
        square[rows, pl.ds(skip, 2048 - skip)] = late[quarter][...]
    for cols in range(0, 2048, 256):
        block = dot(square[...], right_ref[:, pl.ds(cols, 256)])
        for n in range(4 * height // BLK):
            row = 4 * (n // (height // BLK)) + height // BLK * half + n % (height // BLK)
            rows = slice(BLK * n, BLK * n + BLK)
            total[rows, pl.ds(cols, 256)] = block[rows] * mc_ref[pl.ds(row, 1), pl.ds(cols, 256)]

    def add(n):
        block_row = row_of_slot(4 * n, z, core, layer)
        band = block_row // 16 - 4 * col

        @pl.when((band >= 0) & (band < 4))
        def _():
            cols = pl.ds(pl.multiple_of(512 * band + 128 * layer, 128), 128)
            total[:, cols] += 3.0 * square[:, pl.ds(pl.multiple_of(128 * n, 128), 128)].astype(F32)

    lax.fori_loop(0, 16, lambda n, _: add(n), None)

    for share in range(4):
        cols = pl.ds(pl.multiple_of(512 * lax.rem(layer + share, 4), 512), 512)
        outs[share][...] = total[:, cols].astype(outs[share].dtype)


def finish_kernel(s_ref, *refs):
    col, out_ref = s_ref[2], refs[-1]
    height = 128 // HALVES
    for half in range(HALVES):
        own_ref, *got = refs[4 * half : 4 * half + 4]
        for quarter in range(4):
            rows = pl.ds(height * quarter, height)
            total = own_ref[rows, :]
            for ref in got:
                total = total + ref[rows, :].astype(F32)
            start = 128 * lax.rem(col + quarter, 4) + height * half
            out_ref[pl.ds(pl.multiple_of(start, height), height), :] = total.astype(BF)


def shift(array, axis, step, size):
    return lax.ppermute(array, axis, [(i, (i + step) % size) for i in range(size)])


def swap(array):
    return lax.ppermute(array, "row", [(i, i ^ 1) for i in range(16)])


def exchange(parts, axis):
    got = [shift(part, axis, step, 4) for part, step in zip(parts, (1, 2, 3))]
    return got[2], got[1], got[0]


def body(density, pattern_density, pattern_square, pattern_cube):
    row, col, layer = lax.axis_index("row"), lax.axis_index("col"), lax.axis_index("rep")
    where = jnp.stack([row // 2, row % 2, col, layer]).astype(jnp.int32)
    own = lax.dynamic_slice_in_dim(density, 128 * layer, 128, 0)

    rows = pattern_density.astype(BF)
    pairs = [(row, layer) for row in range(16) for layer in range(4)]
    rows = [
        lax.ppermute(
            rows,
            ("row", "rep"),
            [(4 * row + layer, 4 * ((row - 2 * (layer + far)) % 16) + layer) for row, layer in pairs],
        )
        for far in (0, 4)
    ]
    own, rows = lax.optimization_barrier((own, rows))

    def both_ways(up, down):
        return shift(up, "row", 2, 16), shift(down, "row", -2, 16)

    def with_swapped(held):
        return [*held, *(swap(piece) for piece in held)]

    first = both_ways(own, own)
    rows = jnp.concatenate(rows, 0)
    rows = jnp.concatenate([rows, swap(rows), pattern_square.astype(BF)], 0)
    both = lax.all_to_all(jnp.broadcast_to(rows, (16, 80, 64)), ("col", "rep"), 0, 0)
    *first, both = lax.optimization_barrier((*first, both))
    second = both_ways(*first)
    left, mk, mt, ms, mc = call(
        prep_kernel,
        (
            shape(512, 2048),
            shape(64, 2048, dtype=F32),
            shape(64, 2048, dtype=F32),
            shape(16, 2048, dtype=F32),
            shape(16, 2048, dtype=F32),
        ),
        5,
        flops=2 * 200 * 256 * 2048,
        byts=6 << 20,
    )(where, both, pattern_density, pattern_cube, density)

    def multiply(slots, halves, held):
        height, width = 128 // halves, 256 * len(slots)
        return call(
            functools.partial(product_one_kernel, slots, halves, len(held)),
            ((shape(height, width, dtype=F32),) + (shape(height, width),) * 3) * halves,
            3 + len(held),
            [pltpu.VMEM((width, 2048), BF)],
            flops=2 * 512 * 2048 * width,
            byts=2 * 2048 * (512 + width),
        )(where, left, mt, *held)

    def finish_square(slots, halves, half, mine, got):
        height, width = 128 // halves, 256 * len(slots)
        mine = call(
            functools.partial(square_kernel, slots[0], half * (4 // halves)),
            shape(height, width),
            6,
            byts=2 * height * width * 6,
        )(where, ms, mine, *got)
        return mine, *exchange([mine] * 3, "col")

    early = [piece for held in ([own], first[:1], first[1:]) for piece in with_swapped(held)]
    parts = multiply(range(EARLY), 1, early)
    *second, parts = lax.optimization_barrier((*second, parts))
    third = both_ways(*second)
    third, ends, got, second = lax.optimization_barrier(
        (third, (third[0][:64], third[1][64:]), exchange(parts[1:], "col"), second)
    )
    fourth = both_ways(*ends)
    late = [with_swapped(held) for held in (second[:1], second[1:], third[:1], third[1:])]
    late, got = lax.optimization_barrier((late, got))
    early_square = finish_square(range(EARLY), 1, 0, parts[0], got)
    fourth, early_square = lax.optimization_barrier((fourth, early_square))
    late.append(with_swapped(fourth))
    late = [piece for held in late for piece in held]
    slots = range(EARLY, len(SLOTS))
    parts = multiply(slots, HALVES, late)
    parts = [parts[4 * half : 4 * half + 4] for half in range(HALVES)]
    squares = [
        finish_square(slots, HALVES, half, mine, exchange(others, "col")) for half, (mine, *others) in enumerate(parts)
    ]
    right = call(right_kernel, shape(2048, 2048), 2 + len(early + late), byts=16 << 20)(where, mk, *early, *late)
    results = []
    for half in range(HALVES):
        height = 512 // HALVES
        mine, *others = call(
            functools.partial(product_two_kernel, half, len(early_square)),
            (shape(height, 512, dtype=F32),) + (shape(height, 512),) * 3,
            3 + len(early_square) + 4,
            [pltpu.VMEM((height, 2048), BF), pltpu.VMEM((height, 2048), F32)],
            flops=2 * height * 2048 * 2048,
            byts=10 << 20,
        )(where, mc, right, *early_square, *squares[half])
        results += [mine, *exchange(others, "rep")]
    return call(finish_kernel, shape(512, 512), 1 + len(results), byts=3 << 20)(where, *results)


def solution(mesh):
    placed = (P("row", "col"), P("row", "col"), P("row", "col"), P("row", "col"))
    return jax.shard_map(
        body, mesh=mesh, in_specs=placed, out_specs=P("row", ("col", "rep")), check_vma=False
    )
```

```python
import functools

import jax
import jax.numpy as jnp
from jax import lax
from jax.experimental import pallas as pl
from jax.experimental.pallas import tpu as pltpu
from jax.sharding import PartitionSpec as P

BLK = 32
BF = jnp.bfloat16
F32 = jnp.float32
VMEM = pl.BlockSpec(memory_space=pltpu.VMEM)
SMEM = pl.BlockSpec(memory_space=pltpu.SMEM)
NT = (((1,), (1,)), ((), ()))
NN = (((1,), (0,)), ((), ()))

SLOTS = (0, -1, 1, -2, 2, -3, 3, 4)
EARLY = 5
HALVES = 2


def call(kernel, out_shape, n_in, scratch=(), flops=0, byts=0, mib=20, aliases={}):
    return pl.pallas_call(
        kernel,
        out_shape=out_shape,
        in_specs=[SMEM] + [VMEM] * (n_in - 1),
        out_specs=jax.tree.map(lambda _: VMEM, out_shape),
        scratch_shapes=list(scratch),
        input_output_aliases=aliases,
        compiler_params=pltpu.CompilerParams(vmem_limit_bytes=mib << 20),
        cost_estimate=pl.CostEstimate(flops=flops, bytes_accessed=byts, transcendentals=0),
    )


def shape(*dims, dtype=BF):
    return jax.ShapeDtypeStruct(dims, dtype)


def iota(dims, axis):
    return lax.broadcasted_iota(jnp.int32, dims, axis)


def dot(a, b, dims=NN):
    return lax.dot_general(a, b, dims, preferred_element_type=F32)


def row_of_slot(index, z, core, layer):
    slot = index // 8
    other = (index // 4) % 2
    offset = jnp.where(slot == 7, 4, jnp.where(slot % 2 == 1, -((slot + 1) // 2), slot // 2))
    chip = lax.rem(z + offset + 8, 8)
    band = 2 * chip + lax.rem(core + other, 2)
    return 16 * band + 4 * layer + index % 4


def prep_kernel(s_ref, *refs):
    both_ref, local_ref, cube_ref, density_ref, left_ref, mk_ref, mt_ref, ms_ref, mc_ref = refs
    z, core, col, layer = s_ref[0], s_ref[1], s_ref[2], s_ref[3]
    wide = (iota((64, 2048), 0) == iota((64, 2048), 1) // BLK).astype(BF)
    roll = (iota((16, 16), 1) == lax.rem(iota((16, 16), 0) + 4 * col, 16)).astype(BF)
    local = dot(dot(roll, local_ref[...].astype(BF)).astype(BF), wide).astype(BF)
    for quarter in range(4):
        start = pl.multiple_of(128 * lax.rem(col + quarter, 4), 128)
        for block in range(4):
            at = 4 * quarter + block
            left_ref[pl.ds(BLK * at, BLK), :] = (
                density_ref[pl.ds(start + BLK * block, BLK), :] * local[at : at + 1, :]
            )
    at = iota((64, 1280), 1)
    device, inner = at // 80, at % 80
    chip = lax.rem(z + device % 4 + 4 * ((inner // 16) % 2), 8)
    block_row = 16 * (2 * chip + lax.rem(core + inner // 32, 2)) + inner % 16
    density = inner < 64
    both = both_ref[...].reshape(1280, 64)
    pick = density & (block_row == row_of_slot(iota((64, 1280), 0), z, core, layer)) & (device // 4 == col)
    mk = dot(jnp.where(pick, 1.0, 0.0).astype(BF), both).astype(BF)
    mt = jnp.zeros((64, 64), F32)
    ms = jnp.zeros((16, 64), F32)
    order = lax.rem(iota((16, 1280), 0) + 4 * col, 16)
    square_at = iota((16, 1280), 1)
    for n in range(4):
        mine = density & (block_row == 64 * col + iota((64, 1280), 0)) & (device // 4 == n)
        rows = dot(jnp.where(mine, 1.0, 0.0).astype(BF), both).astype(BF)
        column = 64 * n + iota((64, 64), 1)
        take = (column == row_of_slot(iota((64, 64), 0), z, core, layer)).astype(BF)
        mt = mt + dot(take, rows, NT)
        own = square_at == 80 * (4 * n + layer) + 64 + order
        rows = dot(jnp.where(own, 1.0, 0.0).astype(BF), both).astype(BF)
        ms = ms + dot(rows, take, NT)
    mk_ref[...] = dot(mk, wide)
    mt_ref[...] = dot(mt.astype(BF), wide)
    ms_ref[...] = dot(ms.astype(BF), wide)
    mc_ref[...] = -2.0 * dot(dot(roll, cube_ref[...].astype(BF)).astype(BF), wide)


def load_pieces(piece_refs, mask_ref, block_row, out_ref):
    done = 0
    for ref in piece_refs:
        for block in range(ref.shape[0] // BLK):
            row = block_row + done // BLK
            keep = jnp.broadcast_to(mask_ref[pl.ds(row, 1), :], (BLK, 2048)).astype(BF)
            out_ref[pl.ds(done, BLK), :] = ref[pl.ds(BLK * block, BLK), :] * keep
            done += BLK


def product_one_kernel(slots, halves, n_pieces, s_ref, left_ref, mt_ref, *refs):
    pieces, outs, right = refs[:n_pieces], refs[n_pieces:-1], refs[-1]
    load_pieces(pieces, mt_ref, 8 * slots[0], right)
    height = 128 // halves
    for start in range(0, right.shape[0], 256):
        block = dot(left_ref[...], right[pl.ds(start, 256), :], NT)
        for half in range(halves):
            for quarter in range(4):
                row = 128 * quarter + height * half
                out = outs[4 * half + quarter]
                out[:, pl.ds(start, 256)] = block[row : row + height].astype(out.dtype)


def square_kernel(first_slot, first_block, s_ref, ms_ref, own_ref, a_ref, b_ref, c_ref, out_ref):
    height, width = out_ref.shape
    total = own_ref[...] + a_ref[...].astype(F32) + b_ref[...].astype(F32) + c_ref[...].astype(F32)
    for block in range(height // BLK):
        rows = slice(BLK * block, BLK * block + BLK)
        keep = ms_ref[pl.ds(first_block + block, 1), pl.ds(256 * first_slot, width)]
        out_ref[rows, :] = (total[rows] * keep).astype(BF)


def right_kernel(s_ref, mk_ref, *refs):
    load_pieces(refs[:-1], mk_ref, 0, refs[-1])


def product_two_kernel(half, n_early, s_ref, mc_ref, right_ref, *refs):
    z, core, col, layer = s_ref[0], s_ref[1], s_ref[2], s_ref[3]
    early, late, outs = refs[:n_early], refs[n_early : n_early + 4], refs[n_early + 4 : n_early + 8]
    square, total = refs[-2:]
    height = 128 // HALVES
    skip = 256 * EARLY if n_early else 0
    for quarter in range(4):
        rows = pl.ds(height * quarter, height)
        if n_early:
            square[rows, pl.ds(0, skip)] = early[quarter][pl.ds(height * half, height), :]
        square[rows, pl.ds(skip, 2048 - skip)] = late[quarter][...]
    for cols in range(0, 2048, 256):
        block = dot(square[...], right_ref[:, pl.ds(cols, 256)])
        for n in range(4 * height // BLK):
            row = 4 * (n // (height // BLK)) + height // BLK * half + n % (height // BLK)
            rows = slice(BLK * n, BLK * n + BLK)
            total[rows, pl.ds(cols, 256)] = block[rows] * mc_ref[pl.ds(row, 1), pl.ds(cols, 256)]

    def add(n):
        block_row = row_of_slot(4 * n, z, core, layer)
        band = block_row // 16 - 4 * col

        @pl.when((band >= 0) & (band < 4))
        def _():
            cols = pl.ds(pl.multiple_of(512 * band + 128 * layer, 128), 128)
            total[:, cols] += 3.0 * square[:, pl.ds(pl.multiple_of(128 * n, 128), 128)].astype(F32)

    lax.fori_loop(0, 16, lambda n, _: add(n), None)

    for share in range(4):
        cols = pl.ds(pl.multiple_of(512 * lax.rem(layer + share, 4), 512), 512)
        outs[share][...] = total[:, cols].astype(outs[share].dtype)


def finish_kernel(s_ref, *refs):
    col, out_ref = s_ref[2], refs[-1]
    height = 128 // HALVES
    for half in range(HALVES):
        own_ref, *got = refs[4 * half : 4 * half + 4]
        for quarter in range(4):
            rows = pl.ds(height * quarter, height)
            total = own_ref[rows, :]
            for ref in got:
                total = total + ref[rows, :].astype(F32)
            start = 128 * lax.rem(col + quarter, 4) + height * half
            out_ref[pl.ds(pl.multiple_of(start, height), height), :] = total.astype(BF)


def shift(array, axis, step, size):
    return lax.ppermute(array, axis, [(i, (i + step) % size) for i in range(size)])


def swap(array):
    return lax.ppermute(array, "row", [(i, i ^ 1) for i in range(16)])


def exchange(parts, axis):
    got = [shift(part, axis, step, 4) for part, step in zip(parts, (1, 2, 3))]
    return got[2], got[1], got[0]


def with_swapped(held):
    return [*held, *(swap(piece) for piece in held)]


def body(density, pattern_density, pattern_square, pattern_cube):
    row, col, layer = lax.axis_index("row"), lax.axis_index("col"), lax.axis_index("rep")
    where = jnp.stack([row // 2, row % 2, col, layer]).astype(jnp.int32)
    own = lax.dynamic_slice_in_dim(density, 128 * layer, 128, 0)

    rows = pattern_density.astype(BF)
    pairs = [(row, layer) for row in range(16) for layer in range(4)]
    rows = [
        lax.ppermute(
            rows,
            ("row", "rep"),
            [(4 * row + layer, 4 * ((row - 2 * (layer + far)) % 16) + layer) for row, layer in pairs],
        )
        for far in (0, 4)
    ]
    own, rows = lax.optimization_barrier((own, rows))

    def both_ways(up, down):
        return shift(up, "row", 2, 16), shift(down, "row", -2, 16)

    first = both_ways(own, own)
    rows = jnp.concatenate(rows, 0)
    rows = jnp.concatenate([rows, swap(rows), pattern_square.astype(BF)], 0)
    *first, rows = lax.optimization_barrier((*first, jnp.broadcast_to(rows, (16, 80, 64))))
    second = both_ways(*first)
    both = lax.all_to_all(rows, ("col", "rep"), 0, 0)
    early = [piece for one in ([own], first[:1], first[1:]) for piece in with_swapped(one)]
    *second, both, early = lax.optimization_barrier((*second, both, early))
    left, mk, mt, ms, mc = call(
        prep_kernel,
        (
            shape(512, 2048),
            shape(64, 2048, dtype=F32),
            shape(64, 2048, dtype=F32),
            shape(16, 2048, dtype=F32),
            shape(16, 2048, dtype=F32),
        ),
        5,
        flops=2 * 200 * 256 * 2048,
        byts=6 << 20,
    )(where, both, pattern_density, pattern_cube, density)

    def multiply(slots, halves, held):
        height, width = 128 // halves, 256 * len(slots)
        return call(
            functools.partial(product_one_kernel, slots, halves, len(held)),
            ((shape(height, width, dtype=F32),) + (shape(height, width),) * 3) * halves,
            3 + len(held),
            [pltpu.VMEM((width, 2048), BF)],
            flops=2 * 512 * 2048 * width,
            byts=2 * 2048 * (512 + width),
        )(where, left, mt, *held)

    def finish_square(slots, halves, half, mine, got):
        height, width = 128 // halves, 256 * len(slots)
        mine = call(
            functools.partial(square_kernel, slots[0], half * (4 // halves)),
            shape(height, width),
            6,
            byts=2 * height * width * 6,
        )(where, ms, mine, *got)
        return mine, *exchange([mine] * 3, "col")

    third = both_ways(*second)
    early += [piece for one in (second[:1], second[1:]) for piece in with_swapped(one)]
    parts = multiply(range(EARLY), 1, early)
    third, parts = lax.optimization_barrier((third, parts))
    fourth = both_ways(third[0][:64], third[1][64:])
    fourth, third = lax.optimization_barrier((fourth, third))
    late = [with_swapped(one) for one in (third[:1], third[1:])]
    got = exchange(parts[1:], "col")
    early_square = finish_square(range(EARLY), 1, 0, parts[0], got)
    late = [piece for one in (*late, with_swapped(fourth)) for piece in one]
    slots = range(EARLY, len(SLOTS))
    parts = multiply(slots, HALVES, late)
    parts = [parts[4 * half : 4 * half + 4] for half in range(HALVES)]
    squares = [
        finish_square(slots, HALVES, half, mine, exchange(others, "col")) for half, (mine, *others) in enumerate(parts)
    ]
    right = call(right_kernel, shape(2048, 2048), 2 + len(early + late), byts=16 << 20)(where, mk, *early, *late)
    results = []
    for half in range(HALVES):
        height = 512 // HALVES
        mine, *others = call(
            functools.partial(product_two_kernel, half, len(early_square)),
            (shape(height, 512, dtype=F32),) + (shape(height, 512),) * 3,
            3 + len(early_square) + 4,
            [pltpu.VMEM((height, 2048), BF), pltpu.VMEM((height, 2048), F32)],
            flops=2 * height * 2048 * 2048,
            byts=10 << 20,
        )(where, mc, right, *early_square, *squares[half])
        results += [mine, *exchange(others, "rep")]
    return call(finish_kernel, shape(512, 512), 1 + len(results), byts=3 << 20)(where, *results)


def solution(mesh):
    placed = (P("row", "col"), P("row", "col"), P("row", "col"), P("row", "col"))
    return jax.shard_map(
        body, mesh=mesh, in_specs=placed, out_specs=P("row", ("col", "rep")), check_vma=False
    )
```

```python
import functools

import jax
import jax.numpy as jnp
from jax import lax
from jax.experimental import pallas as pl
from jax.experimental.pallas import tpu as pltpu
from jax.sharding import PartitionSpec as P

BLK = 32
BF = jnp.bfloat16
F32 = jnp.float32
VMEM = pl.BlockSpec(memory_space=pltpu.VMEM)
SMEM = pl.BlockSpec(memory_space=pltpu.SMEM)
NT = (((1,), (1,)), ((), ()))
NN = (((1,), (0,)), ((), ()))

SLOTS = (0, -1, 1, -2, 2, -3, 3, 4)
EARLY = 3
HALVES = 2


def call(kernel, out_shape, n_in, scratch=(), flops=0, byts=0, far=False, mib=24):
    return pl.pallas_call(
        kernel,
        out_shape=out_shape,
        in_specs=[SMEM] + [VMEM] * (n_in - 1 - far) + [pl.BlockSpec(memory_space=pl.ANY)] * far,
        out_specs=jax.tree.map(lambda _: VMEM, out_shape),
        scratch_shapes=list(scratch),
        compiler_params=pltpu.CompilerParams(vmem_limit_bytes=mib << 20),
        cost_estimate=pl.CostEstimate(flops=flops, bytes_accessed=byts, transcendentals=0),
    )


def shape(*dims, dtype=BF):
    return jax.ShapeDtypeStruct(dims, dtype)


def iota(dims, axis):
    return lax.broadcasted_iota(jnp.int32, dims, axis)


def dot(a, b, dims=NN):
    return lax.dot_general(a, b, dims, preferred_element_type=F32)


def row_of_slot(index, z, core, layer):
    slot = index // 8
    other = (index // 4) % 2
    offset = jnp.where(slot == 7, 4, jnp.where(slot % 2 == 1, -((slot + 1) // 2), slot // 2))
    chip = lax.rem(z + offset + 8, 8)
    band = 2 * chip + lax.rem(core + other, 2)
    return 16 * band + 4 * layer + index % 4


def prep_kernel(s_ref, *refs):
    both_ref, local_ref, cube_ref, density_ref, left_ref, mk_ref, mt_ref, ms_ref, mc_ref = refs
    z, core, col, layer = s_ref[0], s_ref[1], s_ref[2], s_ref[3]
    wide = (iota((64, 2048), 0) == iota((64, 2048), 1) // BLK).astype(BF)
    roll = (iota((16, 16), 1) == lax.rem(iota((16, 16), 0) + 4 * col, 16)).astype(BF)
    local = dot(dot(roll, local_ref[...].astype(BF)).astype(BF), wide).astype(BF)
    for quarter in range(4):
        start = pl.multiple_of(128 * lax.rem(col + quarter, 4), 128)
        for block in range(4):
            at = 4 * quarter + block
            left_ref[pl.ds(BLK * at, BLK), :] = (
                density_ref[pl.ds(start + BLK * block, BLK), :] * local[at : at + 1, :]
            )
    at = iota((64, 1024), 1)
    block_row = 16 * (at // 64) + at % 16
    mine_too = (at // 16) % 4
    share = row_of_slot(iota((64, 1024), 0), z, core, layer)
    pick = jnp.where((block_row == share) & (mine_too == col), 1.0, 0.0).astype(BF)
    both = both_ref[...].reshape(1024, 128)
    mk = dot(pick, both)[:, :64].astype(BF)
    mt = jnp.zeros((64, 64), F32)
    ms = jnp.zeros((16, 64), F32)
    square_row = iota((16, 1024), 0) + 16 * (2 * z + core)
    square_at = iota((16, 1024), 1)
    square_block = 16 * (square_at // 64) + square_at % 16
    for n in range(4):
        mine = (block_row == 64 * col + iota((64, 1024), 0)) & (mine_too == n)
        rows = dot(jnp.where(mine, 1.0, 0.0).astype(BF), both)[:, :64].astype(BF)
        column = 64 * n + iota((64, 64), 1)
        take = (column == row_of_slot(iota((64, 64), 0), z, core, layer)).astype(BF)
        mt = mt + dot(take, rows, NT)
        own = (square_block == square_row) & ((square_at // 16) % 4 == n)
        rows = dot(jnp.where(own, 1.0, 0.0).astype(BF), both)[:, 64:].astype(BF)
        ms = ms + dot(dot(roll, rows).astype(BF), take, NT)
    mk_ref[...] = dot(mk, wide)
    mt_ref[...] = dot(mt.astype(BF), wide)
    ms_ref[...] = dot(ms.astype(BF), wide)
    mc_ref[...] = -2.0 * dot(dot(roll, cube_ref[...].astype(BF)).astype(BF), wide)


def load_pieces(piece_refs, mask_ref, block_row, out_ref):
    done = 0
    for ref in piece_refs:
        for block in range(ref.shape[0] // BLK):
            row = block_row + done // BLK
            keep = jnp.broadcast_to(mask_ref[pl.ds(row, 1), :], (BLK, 2048)).astype(BF)
            out_ref[pl.ds(done, BLK), :] = ref[pl.ds(BLK * block, BLK), :] * keep
            done += BLK


def fetch_slots(slots, where, gathered_ref, mask_ref, out_ref, sems):
    z, core = where
    copies = []
    for n, slot in enumerate(slots):
        chip = lax.rem(z + SLOTS[slot] + 8, 8)
        for other in range(2):
            start = pl.multiple_of(128 * (2 * chip + lax.rem(core + other, 2)), 128)
            copy = pltpu.make_async_copy(
                gathered_ref.at[pl.ds(start, 128), :],
                out_ref.at[pl.ds(256 * n + 128 * other, 128), :],
                sems.at[2 * n + other],
            )
            copy.start()
            copies.append(copy)

    def mask(n):
        copies[2 * n].wait()
        copies[2 * n + 1].wait()
        for block in range(8):
            keep = mask_ref[pl.ds(8 * slots[n] + block, 1), :]
            rows = pl.ds(256 * n + BLK * block, BLK)
            out_ref[rows, :] = out_ref[rows, :] * jnp.broadcast_to(keep, (BLK, 2048)).astype(BF)

    return mask


def product_one_kernel(slots, halves, n_pieces, s_ref, left_ref, mt_ref, *refs):
    pieces, outs, (right, sems) = refs[:n_pieces], refs[n_pieces:-2], refs[-2:]
    if n_pieces > 1:
        load_pieces(pieces, mt_ref, 8 * slots[0], right)
        mask = lambda n: None
    else:
        mask = fetch_slots(slots, (s_ref[0], s_ref[1]), pieces[0], mt_ref, right, sems)
    height = 128 // halves
    for n in range(len(slots)):
        mask(n)
        block = dot(left_ref[...], right[pl.ds(256 * n, 256), :], NT)
        for half in range(halves):
            for quarter in range(4):
                row = 128 * quarter + height * half
                out = outs[4 * half + quarter]
                out[:, pl.ds(256 * n, 256)] = block[row : row + height].astype(out.dtype)


def square_kernel(first_slot, first_block, s_ref, ms_ref, own_ref, a_ref, b_ref, c_ref, out_ref):
    height, width = out_ref.shape
    total = own_ref[...] + a_ref[...].astype(F32) + b_ref[...].astype(F32) + c_ref[...].astype(F32)
    for block in range(height // BLK):
        rows = slice(BLK * block, BLK * block + BLK)
        keep = ms_ref[pl.ds(first_block + block, 1), pl.ds(256 * first_slot, width)]
        out_ref[rows, :] = (total[rows] * keep).astype(BF)


def right_kernel(s_ref, mk_ref, gathered_ref, out_ref, sems):
    slots = range(len(SLOTS))
    mask = fetch_slots(slots, (s_ref[0], s_ref[1]), gathered_ref, mk_ref, out_ref, sems)
    for n in slots:
        mask(n)


def product_two_kernel(half, n_early, s_ref, mc_ref, right_ref, *refs):
    z, core, col, layer = s_ref[0], s_ref[1], s_ref[2], s_ref[3]
    early, late, outs = refs[:n_early], refs[n_early : n_early + 4], refs[n_early + 4 : n_early + 8]
    square, total = refs[-2:]
    height = 128 // HALVES
    skip = 256 * EARLY if n_early else 0
    for quarter in range(4):
        rows = pl.ds(height * quarter, height)
        if n_early:
            square[rows, pl.ds(0, skip)] = early[quarter][pl.ds(height * half, height), :]
        square[rows, pl.ds(skip, 2048 - skip)] = late[quarter][...]
    for cols in range(0, 2048, 256):
        block = dot(square[...], right_ref[:, pl.ds(cols, 256)])
        for n in range(4 * height // BLK):
            row = 4 * (n // (height // BLK)) + height // BLK * half + n % (height // BLK)
            rows = slice(BLK * n, BLK * n + BLK)
            total[rows, pl.ds(cols, 256)] = block[rows] * mc_ref[pl.ds(row, 1), pl.ds(cols, 256)]
    for slot in range(len(SLOTS)):
        chip = lax.rem(z + SLOTS[slot] + 8, 8)

        @pl.when(chip // 2 == col)
        def _():
            for other in range(2):
                band = 2 * chip + lax.rem(core + other, 2) - 4 * col
                cols = pl.ds(pl.multiple_of(512 * band + 128 * layer, 128), 128)
                total[:, cols] += 3.0 * square[:, pl.ds(256 * slot + 128 * other, 128)].astype(F32)

    for share in range(4):
        cols = pl.ds(pl.multiple_of(512 * lax.rem(layer + share, 4), 512), 512)
        outs[share][...] = total[:, cols].astype(outs[share].dtype)


def finish_kernel(s_ref, *refs):
    col, out_ref = s_ref[2], refs[-1]
    height = 128 // HALVES
    for half in range(HALVES):
        own_ref, *got = refs[4 * half : 4 * half + 4]
        for quarter in range(4):
            rows = pl.ds(height * quarter, height)
            total = own_ref[rows, :]
            for ref in got:
                total = total + ref[rows, :].astype(F32)
            start = 128 * lax.rem(col + quarter, 4) + height * half
            out_ref[pl.ds(pl.multiple_of(start, height), height), :] = total.astype(BF)


def shift(array, axis, step, size):
    return lax.ppermute(array, axis, [(i, (i + step) % size) for i in range(size)])


def swap(array):
    return lax.ppermute(array, "row", [(i, i ^ 1) for i in range(16)])


def exchange(parts, axis):
    got = [shift(part, axis, step, 4) for part, step in zip(parts, (1, 2, 3))]
    return got[2], got[1], got[0]


def gather_patterns(pattern_density, pattern_square):
    both = jnp.concatenate([pattern_density, pattern_square], 1).astype(BF)
    return lax.all_to_all(jnp.broadcast_to(both, (64, 16, 128)), ("row", "col"), 0, 0)


def body(density, pattern_density, pattern_square, pattern_cube):
    row, col, layer = lax.axis_index("row"), lax.axis_index("col"), lax.axis_index("rep")
    where = jnp.stack([row // 2, row % 2, col, layer]).astype(jnp.int32)
    own = lax.dynamic_slice_in_dim(density, 128 * layer, 128, 0)

    gathered = lax.all_gather(own, "row", axis=0, tiled=True)
    near = [own, shift(own, "row", 2, 16), shift(own, "row", -2, 16)][:EARLY]
    early = [piece for one in near for piece in (one, swap(one))]

    both = gather_patterns(pattern_density, pattern_square)
    left, mk, mt, ms, mc = call(
        prep_kernel,
        (
            shape(512, 2048),
            shape(64, 2048, dtype=F32),
            shape(64, 2048, dtype=F32),
            shape(16, 2048, dtype=F32),
            shape(16, 2048, dtype=F32),
        ),
        5,
        flops=2 * 200 * 256 * 2048,
        byts=6 << 20,
    )(where, both, pattern_density, pattern_cube, density)

    def start(slots, halves, held):
        height, width = 128 // halves, 256 * len(slots)
        parts = call(
            functools.partial(product_one_kernel, slots, halves, len(held)),
            ((shape(height, width, dtype=F32),) + (shape(height, width),) * 3) * halves,
            3 + len(held),
            [pltpu.VMEM((width, 2048), BF), pltpu.SemaphoreType.DMA((2 * len(slots),))],
            flops=2 * 512 * 2048 * width,
            byts=2 * 2048 * (512 + width),
            far=len(held) == 1,
            mib=54 if len(held) == 1 else 24,
        )(where, left, mt, *held)
        squares = []
        for half in range(halves):
            mine, *others = parts[4 * half : 4 * half + 4]
            mine = call(
                functools.partial(square_kernel, slots[0], half * (4 // halves)),
                shape(height, width),
                6,
                byts=2 * height * width * 6,
            )(where, ms, mine, *exchange(others, "col"))
            squares.append((mine, *exchange([mine] * 3, "col")))
        return squares

    first = start(range(EARLY), 1, early)[0] if EARLY else ()
    first, gathered = lax.optimization_barrier((first, gathered))
    squares = start(range(EARLY, len(SLOTS)), HALVES, [gathered])
    right = call(
        right_kernel, shape(2048, 2048), 3, [pltpu.SemaphoreType.DMA((2 * len(SLOTS),))], byts=16 << 20, far=True, mib=46
    )(where, mk, gathered)
    results = []
    for half in range(HALVES):
        height = 512 // HALVES
        mine, *others = call(
            functools.partial(product_two_kernel, half, len(first)),
            (shape(height, 512, dtype=F32),) + (shape(height, 512),) * 3,
            3 + len(first) + 4,
            [pltpu.VMEM((height, 2048), BF), pltpu.VMEM((height, 2048), F32)],
            flops=2 * height * 2048 * 2048,
            byts=10 << 20,
        )(where, mc, right, *first, *squares[half])
        results += [mine, *exchange(others, "rep")]
    return call(finish_kernel, shape(512, 512), 1 + len(results), byts=3 << 20)(where, *results)


def solution(mesh):
    placed = (P("row", "col"), P("row", "col"), P("row", "col"), P("row", "col"))
    return jax.shard_map(
        body, mesh=mesh, in_specs=placed, out_specs=P("row", ("col", "rep")), check_vma=False
    )
```

```python
import functools

import jax
import jax.numpy as jnp
from jax import lax
from jax.experimental import pallas as pl
from jax.experimental.pallas import tpu as pltpu
from jax.sharding import PartitionSpec as P

BLK = 32
BF = jnp.bfloat16
F32 = jnp.float32
VMEM = pl.BlockSpec(memory_space=pltpu.VMEM)
SMEM = pl.BlockSpec(memory_space=pltpu.SMEM)
NT = (((1,), (1,)), ((), ()))
NN = (((1,), (0,)), ((), ()))

SLOTS = (0, -1, 1, -2, 2, -3, 3, 4)
EARLY = 3
HALVES = 2


def call(kernel, out_shape, n_in, scratch=(), flops=0, byts=0, mib=24, aliases={}):
    return pl.pallas_call(
        kernel,
        out_shape=out_shape,
        in_specs=[SMEM] + [VMEM] * (n_in - 1),
        out_specs=jax.tree.map(lambda _: VMEM, out_shape),
        scratch_shapes=list(scratch),
        input_output_aliases=aliases,
        compiler_params=pltpu.CompilerParams(vmem_limit_bytes=mib << 20),
        cost_estimate=pl.CostEstimate(flops=flops, bytes_accessed=byts, transcendentals=0),
    )


def shape(*dims, dtype=BF):
    return jax.ShapeDtypeStruct(dims, dtype)


def iota(dims, axis):
    return lax.broadcasted_iota(jnp.int32, dims, axis)


def dot(a, b, dims=NN):
    return lax.dot_general(a, b, dims, preferred_element_type=F32)


def row_of_slot(index, z, core, layer):
    slot = index // 8
    other = (index // 4) % 2
    offset = jnp.where(slot == 7, 4, jnp.where(slot % 2 == 1, -((slot + 1) // 2), slot // 2))
    chip = lax.rem(z + offset + 8, 8)
    band = 2 * chip + lax.rem(core + other, 2)
    return 16 * band + 4 * layer + index % 4


def prep_kernel(s_ref, *refs):
    both_ref, local_ref, cube_ref, density_ref, left_ref, mk_ref, mt_ref, ms_ref, mc_ref = refs
    z, core, col, layer = s_ref[0], s_ref[1], s_ref[2], s_ref[3]
    wide = (iota((64, 2048), 0) == iota((64, 2048), 1) // BLK).astype(BF)
    roll = (iota((16, 16), 1) == lax.rem(iota((16, 16), 0) + 4 * col, 16)).astype(BF)
    local = dot(dot(roll, local_ref[...].astype(BF)).astype(BF), wide).astype(BF)
    for quarter in range(4):
        start = pl.multiple_of(128 * lax.rem(col + quarter, 4), 128)
        for block in range(4):
            at = 4 * quarter + block
            left_ref[pl.ds(BLK * at, BLK), :] = (
                density_ref[pl.ds(start + BLK * block, BLK), :] * local[at : at + 1, :]
            )
    at = iota((64, 1024), 1)
    block_row = 16 * (at // 64) + at % 16
    mine_too = (at // 16) % 4
    share = row_of_slot(iota((64, 1024), 0), z, core, layer)
    pick = jnp.where((block_row == share) & (mine_too == col), 1.0, 0.0).astype(BF)
    both = both_ref[...].reshape(1024, 128)
    mk = dot(pick, both)[:, :64].astype(BF)
    mt = jnp.zeros((64, 64), F32)
    ms = jnp.zeros((16, 64), F32)
    square_row = iota((16, 1024), 0) + 16 * (2 * z + core)
    square_at = iota((16, 1024), 1)
    square_block = 16 * (square_at // 64) + square_at % 16
    for n in range(4):
        mine = (block_row == 64 * col + iota((64, 1024), 0)) & (mine_too == n)
        rows = dot(jnp.where(mine, 1.0, 0.0).astype(BF), both)[:, :64].astype(BF)
        column = 64 * n + iota((64, 64), 1)
        take = (column == row_of_slot(iota((64, 64), 0), z, core, layer)).astype(BF)
        mt = mt + dot(take, rows, NT)
        own = (square_block == square_row) & ((square_at // 16) % 4 == n)
        rows = dot(jnp.where(own, 1.0, 0.0).astype(BF), both)[:, 64:].astype(BF)
        ms = ms + dot(dot(roll, rows).astype(BF), take, NT)
    mk_ref[...] = dot(mk, wide)
    mt_ref[...] = dot(mt.astype(BF), wide)
    ms_ref[...] = dot(ms.astype(BF), wide)
    mc_ref[...] = -2.0 * dot(dot(roll, cube_ref[...].astype(BF)).astype(BF), wide)


def load_pieces(piece_refs, mask_ref, block_row, out_ref):
    done = 0
    for ref in piece_refs:
        for block in range(ref.shape[0] // BLK):
            row = block_row + done // BLK
            keep = jnp.broadcast_to(mask_ref[pl.ds(row, 1), :], (BLK, 2048)).astype(BF)
            out_ref[pl.ds(done, BLK), :] = ref[pl.ds(BLK * block, BLK), :] * keep
            done += BLK


def load_slots(slots, where, gathered_ref, mask_ref, out_ref):
    z, core = where
    for n, slot in enumerate(slots):
        chip = lax.rem(z + SLOTS[slot] + 8, 8)
        for other in range(2):
            start = pl.multiple_of(128 * (2 * chip + lax.rem(core + other, 2)), 128)
            for block in range(4):
                row = 8 * slot + 4 * other + block
                keep = jnp.broadcast_to(mask_ref[pl.ds(row, 1), :], (BLK, 2048)).astype(BF)
                out_ref[pl.ds(256 * n + 128 * other + BLK * block, BLK), :] = (
                    gathered_ref[pl.ds(start + BLK * block, BLK), :] * keep
                )


def product_one_kernel(slots, halves, n_pieces, s_ref, left_ref, mt_ref, *refs):
    pieces, outs, right = refs[:n_pieces], refs[n_pieces:-1], refs[-1]
    if n_pieces > 1:
        load_pieces(pieces, mt_ref, 8 * slots[0], right)
    else:
        load_slots(slots, (s_ref[0], s_ref[1]), pieces[0], mt_ref, right)
    height = 128 // halves
    for start in range(0, right.shape[0], 256):
        block = dot(left_ref[...], right[pl.ds(start, 256), :], NT)
        for half in range(halves):
            for quarter in range(4):
                row = 128 * quarter + height * half
                out = outs[4 * half + quarter]
                out[:, pl.ds(start, 256)] = block[row : row + height].astype(out.dtype)


def square_kernel(first_slot, first_block, s_ref, ms_ref, own_ref, a_ref, b_ref, c_ref, *refs):
    out_ref = refs[-1]
    height, width = out_ref.shape
    total = own_ref[...] + a_ref[...].astype(F32) + b_ref[...].astype(F32) + c_ref[...].astype(F32)
    for block in range(height // BLK):
        rows = slice(BLK * block, BLK * block + BLK)
        keep = ms_ref[pl.ds(first_block + block, 1), pl.ds(256 * first_slot, width)]
        out_ref[rows, :] = (total[rows] * keep).astype(BF)


def right_kernel(s_ref, mk_ref, gathered_ref, out_ref):
    load_slots(range(len(SLOTS)), (s_ref[0], s_ref[1]), gathered_ref, mk_ref, out_ref)


def product_two_kernel(half, n_early, s_ref, mc_ref, right_ref, *refs):
    z, core, col, layer = s_ref[0], s_ref[1], s_ref[2], s_ref[3]
    early, late, outs = refs[:n_early], refs[n_early : n_early + 4], refs[n_early + 4 : n_early + 8]
    square, total = refs[-2:]
    height = 128 // HALVES
    skip = 256 * EARLY if n_early else 0
    for quarter in range(4):
        rows = pl.ds(height * quarter, height)
        if n_early:
            square[rows, pl.ds(0, skip)] = early[quarter][pl.ds(height * half, height), :]
        square[rows, pl.ds(skip, 2048 - skip)] = late[quarter][...]
    for cols in range(0, 2048, 256):
        block = dot(square[...], right_ref[:, pl.ds(cols, 256)])
        for n in range(4 * height // BLK):
            row = 4 * (n // (height // BLK)) + height // BLK * half + n % (height // BLK)
            rows = slice(BLK * n, BLK * n + BLK)
            total[rows, pl.ds(cols, 256)] = block[rows] * mc_ref[pl.ds(row, 1), pl.ds(cols, 256)]
    for slot in range(len(SLOTS)):
        chip = lax.rem(z + SLOTS[slot] + 8, 8)

        @pl.when(chip // 2 == col)
        def _():
            for other in range(2):
                band = 2 * chip + lax.rem(core + other, 2) - 4 * col
                cols = pl.ds(pl.multiple_of(512 * band + 128 * layer, 128), 128)
                total[:, cols] += 3.0 * square[:, pl.ds(256 * slot + 128 * other, 128)].astype(F32)

    for share in range(4):
        cols = pl.ds(pl.multiple_of(512 * lax.rem(layer + share, 4), 512), 512)
        outs[share][...] = total[:, cols].astype(outs[share].dtype)


def finish_kernel(s_ref, *refs):
    col, out_ref = s_ref[2], refs[-1]
    height = 128 // HALVES
    for half in range(HALVES):
        own_ref, *got = refs[4 * half : 4 * half + 4]
        for quarter in range(4):
            rows = pl.ds(height * quarter, height)
            total = own_ref[rows, :]
            for ref in got:
                total = total + ref[rows, :].astype(F32)
            start = 128 * lax.rem(col + quarter, 4) + height * half
            out_ref[pl.ds(pl.multiple_of(start, height), height), :] = total.astype(BF)


def shift(array, axis, step, size):
    return lax.ppermute(array, axis, [(i, (i + step) % size) for i in range(size)])


def swap(array):
    return lax.ppermute(array, "row", [(i, i ^ 1) for i in range(16)])


def exchange(parts, axis):
    got = [shift(part, axis, step, 4) for part, step in zip(parts, (1, 2, 3))]
    return got[2], got[1], got[0]


def gather_patterns(pattern_density, pattern_square):
    both = jnp.concatenate([pattern_density, pattern_square], 1).astype(BF)
    return lax.all_to_all(jnp.broadcast_to(both, (64, 16, 128)), ("row", "col"), 0, 0)


def body(density, pattern_density, pattern_square, pattern_cube):
    row, col, layer = lax.axis_index("row"), lax.axis_index("col"), lax.axis_index("rep")
    where = jnp.stack([row // 2, row % 2, col, layer]).astype(jnp.int32)
    own = lax.dynamic_slice_in_dim(density, 128 * layer, 128, 0)

    gathered = lax.all_gather(own, "row", axis=0, tiled=True)
    near = [own, shift(own, "row", 2, 16), shift(own, "row", -2, 16)][:EARLY]
    early = [piece for one in near for piece in (one, swap(one))]

    both = gather_patterns(pattern_density, pattern_square)
    left, mk, mt, ms, mc = call(
        prep_kernel,
        (
            shape(512, 2048),
            shape(64, 2048, dtype=F32),
            shape(64, 2048, dtype=F32),
            shape(16, 2048, dtype=F32),
            shape(16, 2048, dtype=F32),
        ),
        5,
        flops=2 * 200 * 256 * 2048,
        byts=6 << 20,
    )(where, both, pattern_density, pattern_cube, density)

    def start(slots, halves, held):
        height, width = 128 // halves, 256 * len(slots)
        parts = call(
            functools.partial(product_one_kernel, slots, halves, len(held)),
            ((shape(height, width, dtype=F32),) + (shape(height, width),) * 3) * halves,
            3 + len(held),
            [pltpu.VMEM((width, 2048), BF)],
            flops=2 * 512 * 2048 * width,
            byts=2 * 2048 * (512 + width),
        )(where, left, mt, *held)
        squares = []
        for half in range(halves):
            mine, *others = parts[4 * half : 4 * half + 4]
            mine = call(
                functools.partial(square_kernel, slots[0], half * (4 // halves)),
                shape(height, width),
                8 if halves == 1 else 6,
                byts=2 * height * width * 6,
            )(where, ms, mine, *exchange(others, "col"), *((left, mt) if halves == 1 else ()))
            squares.append((mine, *exchange([mine] * 3, "col")))
        return squares

    first = start(range(EARLY), 1, early)[0] if EARLY else ()
    first, gathered = lax.optimization_barrier((first, gathered))
    squares = start(range(EARLY, len(SLOTS)), HALVES, [gathered])
    right = call(right_kernel, shape(2048, 2048), 3, byts=16 << 20)(where, mk, gathered)
    results = []
    for half in range(HALVES):
        height = 512 // HALVES
        mine, *others = call(
            functools.partial(product_two_kernel, half, len(first)),
            (shape(height, 512, dtype=F32),) + (shape(height, 512),) * 3,
            3 + len(first) + 4,
            [pltpu.VMEM((height, 2048), BF), pltpu.VMEM((height, 2048), F32)],
            flops=2 * height * 2048 * 2048,
            byts=10 << 20,
        )(where, mc, right, *first, *squares[half])
        results += [mine, *exchange(others, "rep")]
    return call(finish_kernel, shape(512, 512), 1 + len(results), byts=3 << 20)(where, *results)


def solution(mesh):
    placed = (P("row", "col"), P("row", "col"), P("row", "col"), P("row", "col"))
    return jax.shard_map(
        body, mesh=mesh, in_specs=placed, out_specs=P("row", ("col", "rep")), check_vma=False
    )
```

```python
import functools

import jax
import jax.numpy as jnp
from jax import lax
from jax.experimental import pallas as pl
from jax.experimental.pallas import tpu as pltpu
from jax.sharding import PartitionSpec as P

BLK = 32
BF = jnp.bfloat16
F32 = jnp.float32
VMEM = pl.BlockSpec(memory_space=pltpu.VMEM)
SMEM = pl.BlockSpec(memory_space=pltpu.SMEM)
NT = (((1,), (1,)), ((), ()))
NN = (((1,), (0,)), ((), ()))

SLOTS = (0, -1, 1, -2, 2, -3, 3, 4)
EARLY = 3
HALVES = 2


def call(kernel, out_shape, n_in, scratch=(), flops=0, byts=0, mib=24, aliases={}):
    return pl.pallas_call(
        kernel,
        out_shape=out_shape,
        in_specs=[SMEM] + [VMEM] * (n_in - 1),
        out_specs=jax.tree.map(lambda _: VMEM, out_shape),
        scratch_shapes=list(scratch),
        input_output_aliases=aliases,
        compiler_params=pltpu.CompilerParams(vmem_limit_bytes=mib << 20),
        cost_estimate=pl.CostEstimate(flops=flops, bytes_accessed=byts, transcendentals=0),
    )


def shape(*dims, dtype=BF):
    return jax.ShapeDtypeStruct(dims, dtype)


def iota(dims, axis):
    return lax.broadcasted_iota(jnp.int32, dims, axis)


def dot(a, b, dims=NN):
    return lax.dot_general(a, b, dims, preferred_element_type=F32)


def row_of_slot(index, z, core, layer):
    slot = index // 8
    other = (index // 4) % 2
    offset = jnp.where(slot == 7, 4, jnp.where(slot % 2 == 1, -((slot + 1) // 2), slot // 2))
    chip = lax.rem(z + offset + 8, 8)
    band = 2 * chip + lax.rem(core + other, 2)
    return 16 * band + 4 * layer + index % 4


def prep_kernel(s_ref, *refs):
    both_ref, local_ref, cube_ref, density_ref, left_ref, mk_ref, mt_ref, ms_ref, mc_ref = refs
    z, core, col, layer = s_ref[0], s_ref[1], s_ref[2], s_ref[3]
    wide = (iota((64, 2048), 0) == iota((64, 2048), 1) // BLK).astype(BF)
    roll = (iota((16, 16), 1) == lax.rem(iota((16, 16), 0) + 4 * col, 16)).astype(BF)
    local = dot(dot(roll, local_ref[...].astype(BF)).astype(BF), wide).astype(BF)
    for quarter in range(4):
        start = pl.multiple_of(128 * lax.rem(col + quarter, 4), 128)
        for block in range(4):
            at = 4 * quarter + block
            left_ref[pl.ds(BLK * at, BLK), :] = (
                density_ref[pl.ds(start + BLK * block, BLK), :] * local[at : at + 1, :]
            )
    at = iota((64, 1024), 1)
    block_row = 16 * (at // 64) + at % 16
    mine_too = (at // 16) % 4
    share = row_of_slot(iota((64, 1024), 0), z, core, layer)
    pick = jnp.where((block_row == share) & (mine_too == col), 1.0, 0.0).astype(BF)
    both = both_ref[...].reshape(1024, 128)
    mk = dot(pick, both)[:, :64].astype(BF)
    mt = jnp.zeros((64, 64), F32)
    ms = jnp.zeros((16, 64), F32)
    square_row = iota((16, 1024), 0) + 16 * (2 * z + core)
    square_at = iota((16, 1024), 1)
    square_block = 16 * (square_at // 64) + square_at % 16
    for n in range(4):
        mine = (block_row == 64 * col + iota((64, 1024), 0)) & (mine_too == n)
        rows = dot(jnp.where(mine, 1.0, 0.0).astype(BF), both)[:, :64].astype(BF)
        column = 64 * n + iota((64, 64), 1)
        take = (column == row_of_slot(iota((64, 64), 0), z, core, layer)).astype(BF)
        mt = mt + dot(take, rows, NT)
        own = (square_block == square_row) & ((square_at // 16) % 4 == n)
        rows = dot(jnp.where(own, 1.0, 0.0).astype(BF), both)[:, 64:].astype(BF)
        ms = ms + dot(dot(roll, rows).astype(BF), take, NT)
    mk_ref[...] = dot(mk, wide)
    mt_ref[...] = dot(mt.astype(BF), wide)
    ms_ref[...] = dot(ms.astype(BF), wide)
    mc_ref[...] = -2.0 * dot(dot(roll, cube_ref[...].astype(BF)).astype(BF), wide)


def load_pieces(piece_refs, mask_ref, block_row, out_ref):
    done = 0
    for ref in piece_refs:
        for block in range(ref.shape[0] // BLK):
            row = block_row + done // BLK
            keep = jnp.broadcast_to(mask_ref[pl.ds(row, 1), :], (BLK, 2048)).astype(BF)
            out_ref[pl.ds(done, BLK), :] = ref[pl.ds(BLK * block, BLK), :] * keep
            done += BLK


def load_slots(slots, where, gathered_ref, mask_ref, out_ref):
    z, core = where
    for n, slot in enumerate(slots):
        chip = lax.rem(z + SLOTS[slot] + 8, 8)
        for other in range(2):
            start = pl.multiple_of(128 * (2 * chip + lax.rem(core + other, 2)), 128)
            for block in range(4):
                row = 8 * slot + 4 * other + block
                keep = jnp.broadcast_to(mask_ref[pl.ds(row, 1), :], (BLK, 2048)).astype(BF)
                out_ref[pl.ds(256 * n + 128 * other + BLK * block, BLK), :] = (
                    gathered_ref[pl.ds(start + BLK * block, BLK), :] * keep
                )


def product_one_kernel(slots, halves, half, n_pieces, s_ref, left_ref, mt_ref, *refs):
    pieces, outs, right = refs[:n_pieces], refs[n_pieces:-1], refs[-1]
    if n_pieces > 1:
        load_pieces(pieces, mt_ref, 8 * slots[0], right)
    else:
        load_slots(slots, (s_ref[0], s_ref[1]), pieces[0], mt_ref, right)
    height = 128 // halves
    left = jnp.concatenate([left_ref[pl.ds(128 * quarter + height * half, height), :] for quarter in range(4)], 0)
    for start in range(0, right.shape[0], 256):
        block = dot(left, right[pl.ds(start, 256), :], NT)
        for quarter in range(4):
            rows = slice(height * quarter, height * quarter + height)
            outs[quarter][:, pl.ds(start, 256)] = block[rows].astype(outs[quarter].dtype)


def square_kernel(first_slot, first_block, s_ref, ms_ref, own_ref, a_ref, b_ref, c_ref, *refs):
    out_ref = refs[-1]
    height, width = out_ref.shape
    total = own_ref[...] + a_ref[...].astype(F32) + b_ref[...].astype(F32) + c_ref[...].astype(F32)
    for block in range(height // BLK):
        rows = slice(BLK * block, BLK * block + BLK)
        keep = ms_ref[pl.ds(first_block + block, 1), pl.ds(256 * first_slot, width)]
        out_ref[rows, :] = (total[rows] * keep).astype(BF)


def right_kernel(s_ref, mk_ref, gathered_ref, out_ref):
    load_slots(range(len(SLOTS)), (s_ref[0], s_ref[1]), gathered_ref, mk_ref, out_ref)


def product_two_kernel(half, n_early, s_ref, mc_ref, right_ref, *refs):
    z, core, col, layer = s_ref[0], s_ref[1], s_ref[2], s_ref[3]
    early, late, outs = refs[:n_early], refs[n_early : n_early + 4], refs[n_early + 4 : n_early + 8]
    square, total = refs[-2:]
    height = 128 // HALVES
    skip = 256 * EARLY if n_early else 0
    for quarter in range(4):
        rows = pl.ds(height * quarter, height)
        if n_early:
            square[rows, pl.ds(0, skip)] = early[quarter][pl.ds(height * half, height), :]
        square[rows, pl.ds(skip, 2048 - skip)] = late[quarter][...]
    for cols in range(0, 2048, 256):
        block = dot(square[...], right_ref[:, pl.ds(cols, 256)])
        for n in range(4 * height // BLK):
            row = 4 * (n // (height // BLK)) + height // BLK * half + n % (height // BLK)
            rows = slice(BLK * n, BLK * n + BLK)
            total[rows, pl.ds(cols, 256)] = block[rows] * mc_ref[pl.ds(row, 1), pl.ds(cols, 256)]
    for slot in range(len(SLOTS)):
        chip = lax.rem(z + SLOTS[slot] + 8, 8)

        @pl.when(chip // 2 == col)
        def _():
            for other in range(2):
                band = 2 * chip + lax.rem(core + other, 2) - 4 * col
                cols = pl.ds(pl.multiple_of(512 * band + 128 * layer, 128), 128)
                total[:, cols] += 3.0 * square[:, pl.ds(256 * slot + 128 * other, 128)].astype(F32)

    for share in range(4):
        cols = pl.ds(pl.multiple_of(512 * lax.rem(layer + share, 4), 512), 512)
        outs[share][...] = total[:, cols].astype(outs[share].dtype)


def finish_kernel(s_ref, *refs):
    col, out_ref = s_ref[2], refs[-1]
    height = 128 // HALVES
    for half in range(HALVES):
        own_ref, *got = refs[4 * half : 4 * half + 4]
        for quarter in range(4):
            rows = pl.ds(height * quarter, height)
            total = own_ref[rows, :]
            for ref in got:
                total = total + ref[rows, :].astype(F32)
            start = 128 * lax.rem(col + quarter, 4) + height * half
            out_ref[pl.ds(pl.multiple_of(start, height), height), :] = total.astype(BF)


def shift(array, axis, step, size):
    return lax.ppermute(array, axis, [(i, (i + step) % size) for i in range(size)])


def swap(array):
    return lax.ppermute(array, "row", [(i, i ^ 1) for i in range(16)])


def exchange(parts, axis):
    got = [shift(part, axis, step, 4) for part, step in zip(parts, (1, 2, 3))]
    return got[2], got[1], got[0]


def gather_patterns(pattern_density, pattern_square):
    both = jnp.concatenate([pattern_density, pattern_square], 1).astype(BF)
    return lax.all_to_all(jnp.broadcast_to(both, (64, 16, 128)), ("row", "col"), 0, 0)


def body(density, pattern_density, pattern_square, pattern_cube):
    row, col, layer = lax.axis_index("row"), lax.axis_index("col"), lax.axis_index("rep")
    where = jnp.stack([row // 2, row % 2, col, layer]).astype(jnp.int32)
    own = lax.dynamic_slice_in_dim(density, 128 * layer, 128, 0)

    gathered = lax.all_gather(own, "row", axis=0, tiled=True)
    near = [own, shift(own, "row", 2, 16), shift(own, "row", -2, 16)][:EARLY]
    early = [piece for one in near for piece in (one, swap(one))]

    both = gather_patterns(pattern_density, pattern_square)
    left, mk, mt, ms, mc = call(
        prep_kernel,
        (
            shape(512, 2048),
            shape(64, 2048, dtype=F32),
            shape(64, 2048, dtype=F32),
            shape(16, 2048, dtype=F32),
            shape(16, 2048, dtype=F32),
        ),
        5,
        flops=2 * 200 * 256 * 2048,
        byts=6 << 20,
    )(where, both, pattern_density, pattern_cube, density)

    def start(slots, halves, held):
        height, width = 128 // halves, 256 * len(slots)
        squares = []
        for half in range(halves):
            mine, *others = call(
                functools.partial(product_one_kernel, slots, halves, half, len(held)),
                (shape(height, width, dtype=F32),) + (shape(height, width),) * 3,
                3 + len(held),
                [pltpu.VMEM((width, 2048), BF)],
                flops=2 * 512 // halves * 2048 * width,
                byts=2 * 2048 * (512 + width),
            )(where, left, mt, *held)
            mine = call(
                functools.partial(square_kernel, slots[0], half * (4 // halves)),
                shape(height, width),
                8 if halves == 1 else 6,
                byts=2 * height * width * 6,
            )(where, ms, mine, *exchange(others, "col"), *((left, mt) if halves == 1 else ()))
            squares.append((mine, *exchange([mine] * 3, "col")))
        return squares

    first = start(range(EARLY), 1, early)[0] if EARLY else ()
    first, gathered = lax.optimization_barrier((first, gathered))
    squares = start(range(EARLY, len(SLOTS)), HALVES, [gathered])
    right = call(right_kernel, shape(2048, 2048), 3, byts=16 << 20)(where, mk, gathered)
    results = []
    for half in range(HALVES):
        height = 512 // HALVES
        mine, *others = call(
            functools.partial(product_two_kernel, half, len(first)),
            (shape(height, 512, dtype=F32),) + (shape(height, 512),) * 3,
            3 + len(first) + 4,
            [pltpu.VMEM((height, 2048), BF), pltpu.VMEM((height, 2048), F32)],
            flops=2 * height * 2048 * 2048,
            byts=10 << 20,
        )(where, mc, right, *first, *squares[half])
        results += [mine, *exchange(others, "rep")]
    return call(finish_kernel, shape(512, 512), 1 + len(results), byts=3 << 20)(where, *results)


def solution(mesh):
    placed = (P("row", "col"), P("row", "col"), P("row", "col"), P("row", "col"))
    return jax.shard_map(
        body, mesh=mesh, in_specs=placed, out_specs=P("row", ("col", "rep")), check_vma=False
    )
```

```python
import functools

import jax
import jax.numpy as jnp
from jax import lax
from jax.experimental import pallas as pl
from jax.experimental.pallas import tpu as pltpu
from jax.sharding import PartitionSpec as P

BLK = 32
BF = jnp.bfloat16
F32 = jnp.float32
VMEM = pl.BlockSpec(memory_space=pltpu.VMEM)
SMEM = pl.BlockSpec(memory_space=pltpu.SMEM)
NT = (((1,), (1,)), ((), ()))
NN = (((1,), (0,)), ((), ()))

SLOTS = (0, -1, 1, -2, 2, -3, 3, 4)
EARLY = 3
HALVES = 2


def call(kernel, out_shape, n_in, scratch=(), flops=0, byts=0, mib=16, aliases={}):
    return pl.pallas_call(
        kernel,
        out_shape=out_shape,
        in_specs=[SMEM] + [VMEM] * (n_in - 1),
        out_specs=jax.tree.map(lambda _: VMEM, out_shape),
        scratch_shapes=list(scratch),
        input_output_aliases=aliases,
        compiler_params=pltpu.CompilerParams(vmem_limit_bytes=mib << 20),
        cost_estimate=pl.CostEstimate(flops=flops, bytes_accessed=byts, transcendentals=0),
    )


def shape(*dims, dtype=BF):
    return jax.ShapeDtypeStruct(dims, dtype)


def iota(dims, axis):
    return lax.broadcasted_iota(jnp.int32, dims, axis)


def dot(a, b, dims=NN):
    return lax.dot_general(a, b, dims, preferred_element_type=F32)


def row_of_slot(index, z, core, layer):
    slot = index // 8
    other = (index // 4) % 2
    offset = jnp.where(slot == 7, 4, jnp.where(slot % 2 == 1, -((slot + 1) // 2), slot // 2))
    chip = lax.rem(z + offset + 8, 8)
    band = 2 * chip + lax.rem(core + other, 2)
    return 16 * band + 4 * layer + index % 4


def prep_kernel(s_ref, *refs):
    both_ref, local_ref, cube_ref, density_ref, left_ref, mk_ref, mt_ref, ms_ref, mc_ref = refs
    z, core, col, layer = s_ref[0], s_ref[1], s_ref[2], s_ref[3]
    wide = (iota((64, 2048), 0) == iota((64, 2048), 1) // BLK).astype(BF)
    roll = (iota((16, 16), 1) == lax.rem(iota((16, 16), 0) + 4 * col, 16)).astype(BF)
    local = dot(dot(roll, local_ref[...].astype(BF)).astype(BF), wide).astype(BF)
    for quarter in range(4):
        start = pl.multiple_of(128 * lax.rem(col + quarter, 4), 128)
        for block in range(4):
            at = 4 * quarter + block
            left_ref[pl.ds(BLK * at, BLK), :] = (
                density_ref[pl.ds(start + BLK * block, BLK), :] * local[at : at + 1, :]
            )
    at = iota((64, 1024), 1)
    block_row = 16 * (at // 64) + at % 16
    mine_too = (at // 16) % 4
    share = row_of_slot(iota((64, 1024), 0), z, core, layer)
    pick = jnp.where((block_row == share) & (mine_too == col), 1.0, 0.0).astype(BF)
    both = both_ref[...].reshape(1024, 128)
    mk = dot(pick, both)[:, :64].astype(BF)
    mt = jnp.zeros((64, 64), F32)
    ms = jnp.zeros((16, 64), F32)
    square_row = iota((16, 1024), 0) + 16 * (2 * z + core)
    square_at = iota((16, 1024), 1)
    square_block = 16 * (square_at // 64) + square_at % 16
    for n in range(4):
        mine = (block_row == 64 * col + iota((64, 1024), 0)) & (mine_too == n)
        rows = dot(jnp.where(mine, 1.0, 0.0).astype(BF), both)[:, :64].astype(BF)
        column = 64 * n + iota((64, 64), 1)
        take = (column == row_of_slot(iota((64, 64), 0), z, core, layer)).astype(BF)
        mt = mt + dot(take, rows, NT)
        own = (square_block == square_row) & ((square_at // 16) % 4 == n)
        rows = dot(jnp.where(own, 1.0, 0.0).astype(BF), both)[:, 64:].astype(BF)
        ms = ms + dot(dot(roll, rows).astype(BF), take, NT)
    mk_ref[...] = dot(mk, wide)
    mt_ref[...] = dot(mt.astype(BF), wide)
    ms_ref[...] = dot(ms.astype(BF), wide)
    mc_ref[...] = -2.0 * dot(dot(roll, cube_ref[...].astype(BF)).astype(BF), wide)


def load_pieces(piece_refs, mask_ref, block_row, out_ref):
    done = 0
    for ref in piece_refs:
        for block in range(ref.shape[0] // BLK):
            row = block_row + done // BLK
            keep = jnp.broadcast_to(mask_ref[pl.ds(row, 1), :], (BLK, 2048)).astype(BF)
            out_ref[pl.ds(done, BLK), :] = ref[pl.ds(BLK * block, BLK), :] * keep
            done += BLK


def load_slots(slots, where, gathered_ref, mask_ref, out_ref):
    z, core = where
    for n, slot in enumerate(slots):
        chip = lax.rem(z + SLOTS[slot] + 8, 8)
        for other in range(2):
            start = pl.multiple_of(128 * (2 * chip + lax.rem(core + other, 2)), 128)
            for block in range(4):
                row = 8 * slot + 4 * other + block
                keep = jnp.broadcast_to(mask_ref[pl.ds(row, 1), :], (BLK, 2048)).astype(BF)
                out_ref[pl.ds(256 * n + 128 * other + BLK * block, BLK), :] = (
                    gathered_ref[pl.ds(start + BLK * block, BLK), :] * keep
                )


def product_one_kernel(slots, halves, half, n_pieces, s_ref, left_ref, mt_ref, *refs):
    pieces, outs, right = refs[:n_pieces], refs[n_pieces:-1], refs[-1]
    if n_pieces > 1:
        load_pieces(pieces, mt_ref, 8 * slots[0], right)
    else:
        load_slots(slots, (s_ref[0], s_ref[1]), pieces[0], mt_ref, right)
    height = 128 // halves
    left = jnp.concatenate([left_ref[pl.ds(128 * quarter + height * half, height), :] for quarter in range(4)], 0)
    for start in range(0, right.shape[0], 256):
        block = dot(left, right[pl.ds(start, 256), :], NT)
        for quarter in range(4):
            rows = slice(height * quarter, height * quarter + height)
            outs[quarter][:, pl.ds(start, 256)] = block[rows].astype(outs[quarter].dtype)


def square_kernel(first_slot, first_block, s_ref, ms_ref, own_ref, a_ref, b_ref, c_ref, *refs):
    out_ref = refs[-1]
    height, width = out_ref.shape
    total = own_ref[...] + a_ref[...].astype(F32) + b_ref[...].astype(F32) + c_ref[...].astype(F32)
    for block in range(height // BLK):
        rows = slice(BLK * block, BLK * block + BLK)
        keep = ms_ref[pl.ds(first_block + block, 1), pl.ds(256 * first_slot, width)]
        out_ref[rows, :] = (total[rows] * keep).astype(BF)


def right_kernel(s_ref, mk_ref, gathered_ref, out_ref):
    load_slots(range(len(SLOTS)), (s_ref[0], s_ref[1]), gathered_ref, mk_ref, out_ref)


def product_two_kernel(half, n_early, s_ref, mc_ref, right_ref, *refs):
    z, core, col, layer = s_ref[0], s_ref[1], s_ref[2], s_ref[3]
    early, late, outs = refs[:n_early], refs[n_early : n_early + 4], refs[n_early + 4 : n_early + 8]
    square, total = refs[-2:]
    height = 128 // HALVES
    skip = 256 * EARLY if n_early else 0
    for quarter in range(4):
        rows = pl.ds(height * quarter, height)
        if n_early:
            square[rows, pl.ds(0, skip)] = early[quarter][pl.ds(height * half, height), :]
        square[rows, pl.ds(skip, 2048 - skip)] = late[quarter][...]
    for cols in range(0, 2048, 256):
        block = dot(square[...], right_ref[:, pl.ds(cols, 256)])
        for n in range(4 * height // BLK):
            row = 4 * (n // (height // BLK)) + height // BLK * half + n % (height // BLK)
            rows = slice(BLK * n, BLK * n + BLK)
            total[rows, pl.ds(cols, 256)] = block[rows] * mc_ref[pl.ds(row, 1), pl.ds(cols, 256)]
    for slot in range(len(SLOTS)):
        chip = lax.rem(z + SLOTS[slot] + 8, 8)

        @pl.when(chip // 2 == col)
        def _():
            for other in range(2):
                band = 2 * chip + lax.rem(core + other, 2) - 4 * col
                cols = pl.ds(pl.multiple_of(512 * band + 128 * layer, 128), 128)
                total[:, cols] += 3.0 * square[:, pl.ds(256 * slot + 128 * other, 128)].astype(F32)

    for share in range(4):
        cols = pl.ds(pl.multiple_of(512 * lax.rem(layer + share, 4), 512), 512)
        outs[share][...] = total[:, cols].astype(outs[share].dtype)


def finish_kernel(s_ref, *refs):
    col, out_ref = s_ref[2], refs[-1]
    height = 128 // HALVES
    for half in range(HALVES):
        own_ref, *got = refs[4 * half : 4 * half + 4]
        for quarter in range(4):
            rows = pl.ds(height * quarter, height)
            total = own_ref[rows, :]
            for ref in got:
                total = total + ref[rows, :].astype(F32)
            start = 128 * lax.rem(col + quarter, 4) + height * half
            out_ref[pl.ds(pl.multiple_of(start, height), height), :] = total.astype(BF)


def shift(array, axis, step, size):
    return lax.ppermute(array, axis, [(i, (i + step) % size) for i in range(size)])


def swap(array):
    return lax.ppermute(array, "row", [(i, i ^ 1) for i in range(16)])


def exchange(parts, axis):
    got = [shift(part, axis, step, 4) for part, step in zip(parts, (1, 2, 3))]
    return got[2], got[1], got[0]


def gather_patterns(pattern_density, pattern_square):
    both = jnp.concatenate([pattern_density, pattern_square], 1).astype(BF)
    return lax.all_to_all(jnp.broadcast_to(both, (64, 16, 128)), ("row", "col"), 0, 0)


def body(density, pattern_density, pattern_square, pattern_cube):
    row, col, layer = lax.axis_index("row"), lax.axis_index("col"), lax.axis_index("rep")
    where = jnp.stack([row // 2, row % 2, col, layer]).astype(jnp.int32)
    own = lax.dynamic_slice_in_dim(density, 128 * layer, 128, 0)

    gathered = lax.all_gather(own, "row", axis=0, tiled=True)
    near = [own, shift(own, "row", 2, 16), shift(own, "row", -2, 16)][:EARLY]
    early = [piece for one in near for piece in (one, swap(one))]

    both = gather_patterns(pattern_density, pattern_square)
    left, mk, mt, ms, mc = call(
        prep_kernel,
        (
            shape(512, 2048),
            shape(64, 2048, dtype=F32),
            shape(64, 2048, dtype=F32),
            shape(16, 2048, dtype=F32),
            shape(16, 2048, dtype=F32),
        ),
        5,
        flops=2 * 200 * 256 * 2048,
        byts=6 << 20,
    )(where, both, pattern_density, pattern_cube, density)

    def start(slots, halves, held):
        height, width = 128 // halves, 256 * len(slots)
        squares = []
        for half in range(halves):
            mine, *others = call(
                functools.partial(product_one_kernel, slots, halves, half, len(held)),
                (shape(height, width, dtype=F32),) + (shape(height, width),) * 3,
                3 + len(held),
                [pltpu.VMEM((width, 2048), BF)],
                flops=2 * 512 // halves * 2048 * width,
                byts=2 * 2048 * (512 + width),
            )(where, left, mt, *held)
            mine = call(
                functools.partial(square_kernel, slots[0], half * (4 // halves)),
                shape(height, width),
                8 if halves == 1 else 6,
                byts=2 * height * width * 6,
            )(where, ms, mine, *exchange(others, "col"), *((left, mt) if halves == 1 else ()))
            squares.append((mine, *exchange([mine] * 3, "col")))
        return squares

    first = start(range(EARLY), 1, early)[0] if EARLY else ()
    first, gathered = lax.optimization_barrier((first, gathered))
    squares = start(range(EARLY, len(SLOTS)), HALVES, [gathered])
    right = call(right_kernel, shape(2048, 2048), 3, byts=16 << 20)(where, mk, gathered)
    results = []
    for half in range(HALVES):
        height = 512 // HALVES
        mine, *others = call(
            functools.partial(product_two_kernel, half, len(first)),
            (shape(height, 512, dtype=F32),) + (shape(height, 512),) * 3,
            3 + len(first) + 4,
            [pltpu.VMEM((height, 2048), BF), pltpu.VMEM((height, 2048), F32)],
            flops=2 * height * 2048 * 2048,
            byts=10 << 20,
        )(where, mc, right, *first, *squares[half])
        results += [mine, *exchange(others, "rep")]
    return call(finish_kernel, shape(512, 512), 1 + len(results), byts=3 << 20)(where, *results)


def solution(mesh):
    placed = (P("row", "col"), P("row", "col"), P("row", "col"), P("row", "col"))
    return jax.shard_map(
        body, mesh=mesh, in_specs=placed, out_specs=P("row", ("col", "rep")), check_vma=False
    )
```
